256 devices in a mesh: inplane: 8 (over x_hi, y), row: 32 (over x_lo, z, core).
Axes of the slice: x: 4 (x_hi: 2, x_lo: 2; x = x_hi * 2 + x_lo), y: 4, z: 8, core: 2. Of those that a mesh axis runs over, the one named last changes fastest.
Arguments:
- amplitudes: float32 [1024, 1024], P('row'), may hold values from -6 to 6
- previous: float32 [1024, 1024], P('row'), may hold values from -6 to 6
- coupling: bfloat16 [1024, 1024, 1024], P('inplane', 'row'), may hold values from -0.1875 to 0.1875
- stiffness: float32 [1024], replicated, may hold values from 0.01 to 3
- airy_scale: float32 [1024], P('inplane'), may hold values from 256 to 2560
- damping: float32 [1024], replicated, may hold values from 0.01 to 0.5
- strike_mode: int32 [1024], P('row'), may hold values from 0 to 1023
- strike_offset: int32 [1024], P('row'), may hold values from 0 to 127
Outputs:
- next_amplitudes: float32 [1024, 1024], P('row')
- airy: float32 [1024, 1024], P(None, 'inplane')
The draws below stay inside these ranges and needn't reach their ends.
All inputs are finite; a program needn't handle non-finite values.
Results may differ from the reference program's by a relative error of at most 0.0047.
Values may be sent and summed in bfloat16 or wider, within the bound.
No kernel may reach another device: no remote copies, remote signals or barrier semaphores. Data moves between devices by JAX's collectives and lax.ppermute only.
A program may use at most 128 MiB of HBM per device.

```python
import math
import jax
import jax.numpy as jnp
from jax import lax

NW = 1024
NPHI = 1024
STRIKE_LEN = 64
CASES = 1024
N_INPLANE = 8


def place_ends(values, own_key, smallest, high):
    longest = values.shape.index(max(values.shape))
    spots = []
    for shift in (0, 1):
        where = [jax.random.randint(jax.random.fold_in(own_key, axis), (), 0, length) for axis, length in enumerate(values.shape)]
        where[longest] = (where[longest] + shift) % values.shape[longest]
        spots.append(tuple(where))
    return values.at[spots[0]].set(smallest).at[spots[1]].set(high)


def levels(rng, dims, cuts, smallest, high):
    def one(axis_at, shards_of):
        draws = jax.random.uniform(jax.random.fold_in(jax.random.fold_in(rng, 6), axis_at), (shards_of,), jnp.float32, smallest / len(cuts), high / len(cuts))
        return jnp.repeat(jnp.exp(draws), dims[axis_at] // shards_of).reshape((-1,) + (1,) * (len(dims) - axis_at - 1))

    level = one(*cuts[0])
    for cut in cuts[1:]:
        level = level * one(*cut)
    return level


def scatter_about(own_key, dims, deviation, most, split=(), kind=jnp.bfloat16):
    level = levels(own_key, dims, split, -0.22, 0.18) if split else 1.0
    drawn = jax.random.normal(own_key, dims, jnp.float32) * deviation * level
    return jnp.minimum(jnp.maximum(drawn, -most), most).astype(kind)


def setup_inputs(seed: int = 0) -> dict:
    key_of = jax.random.split(jax.random.key(seed), 9)
    return {
        "amplitudes": scatter_about(key_of[0], (CASES, NW), 1.0, 6.0, ((0, 32),), jnp.float32),
        "previous": scatter_about(key_of[1], (CASES, NW), 1.0, 6.0, ((0, 32),), jnp.float32),
        "coupling": scatter_about(key_of[2], (NPHI, NW, NW), NW ** -0.5, 0.1875, ((0, 8), (1, 32))),
        "stiffness": jnp.clip(jnp.exp(jax.random.uniform(key_of[3], (NW,), jnp.float32, math.log(0.01), math.log(3.0))), 0.01, 3.0),
        "airy_scale": jnp.clip(jnp.exp(math.log(2560.0) - 2.3025851 * jax.random.uniform(key_of[4], (NPHI,), jnp.float32) ** levels(key_of[4], (NPHI,), ((0, 8),), -0.2, 0.2)), 256.0, 2560.0),
        "damping": jnp.clip(jnp.exp(jax.random.uniform(key_of[5], (NW,), jnp.float32, math.log(0.01), math.log(0.5))), 0.01, 0.5),
        "strike_mode": place_ends(jax.random.randint(key_of[6], (CASES,), 0, NW), jax.random.fold_in(key_of[6], 1), 0, NW - 1).astype(jnp.int32),
        "strike_offset": place_ends(jax.random.randint(key_of[7], (CASES,), 0, 2 * STRIKE_LEN), jax.random.fold_in(key_of[7], 1), 0, (2 * STRIKE_LEN) - 1).astype(jnp.int32),
    }


def reference(amplitudes, previous, coupling, stiffness, airy_scale, damping, strike_mode, strike_offset):
    block = NPHI // N_INPLANE
    rounded = amplitudes.astype(jnp.bfloat16)
    widened = rounded.astype(jnp.float32)
    tensor = coupling.reshape(N_INPLANE, block * NW, NW)
    scales = airy_scale.reshape(N_INPLANE, block)

    def step(total, pair):
        slab, scale = pair
        inner = jnp.dot(slab, rounded.T, preferred_element_type=jnp.float32).reshape(block, NW, CASES)
        coeff = jnp.einsum('kpc,cp->kc', inner, widened) / scale[:, None]
        total = total + jnp.einsum('kc,kpc->cp', coeff, inner)
        return total, coeff.T

    force, pieces = lax.scan(step, jnp.zeros((CASES, NW), jnp.float32), (tensor, scales))
    airy = jnp.transpose(pieces, (1, 0, 2)).reshape(CASES, NPHI)
    offset = strike_offset.astype(jnp.float32)
    pulse = jnp.where(strike_offset <= STRIKE_LEN, 2.0 * (1.0 - jnp.cos(jnp.pi * offset / STRIKE_LEN)), 0.0)
    modes = jnp.arange(NW, dtype=jnp.int32)
    excite = jnp.where(modes[None, :] == strike_mode[:, None], pulse[:, None], 0.0)
    result = (2.0 * amplitudes - (1.0 - damping) * previous - stiffness * amplitudes - force + excite) / (1.0 + damping)
    return result, airy
```

```python
import functools

import jax
import jax.numpy as jnp
from jax import lax
from jax.experimental import pallas as pl
from jax.experimental.pallas import tpu as pltpu
from jax.sharding import Mesh, PartitionSpec as P

STRIKE_LEN = 64
AXES = ("xh", "y", "xl", "z", "c")
SIZES = (2, 4, 2, 8, 2)
INPLANE = ("xh", "y")
ROW = ("xl", "z", "c")
SAME = ("xl", "z")
N_IN = 8
N_SAME = 16
BF = jnp.bfloat16
F32 = jnp.float32


def inner_kernel(row_ref, tensor_ref, cases_ref, inner_ref, part_ref, turned):
    blocks, cases, depth = cases_ref.shape
    slabs, rows, width = tensor_ref.shape

    @pl.when(pl.program_id(0) == 0)
    def _():
        for i in range(blocks):
            turned[i * depth : (i + 1) * depth, :] = cases_ref[i].T

    start = pl.multiple_of(row_ref[0] * rows, rows)
    columns = turned[pl.ds(start, rows), :].astype(F32)
    inner = jnp.dot(
        tensor_ref[...].reshape(slabs * rows, width), turned[...], preferred_element_type=F32
    ).reshape(slabs, rows, cases)
    inner_ref[...] = inner.astype(BF)
    part_ref[...] = jnp.sum(inner * columns[None], axis=1)


def inner_products(row, coupling, cases, slabs=32):
    n_k, rows, width = coupling.shape
    blocks, n_c, depth = cases.shape
    return pl.pallas_call(
        inner_kernel,
        grid_spec=pltpu.PrefetchScalarGridSpec(
            num_scalar_prefetch=1,
            grid=(n_k // slabs,),
            in_specs=[
                pl.BlockSpec((slabs, rows, width), lambda k, r: (k, 0, 0)),
                pl.BlockSpec((blocks, n_c, depth), lambda k, r: (0, 0, 0)),
            ],
            out_specs=[
                pl.BlockSpec((slabs, rows, n_c), lambda k, r: (k, 0, 0)),
                pl.BlockSpec((slabs, n_c), lambda k, r: (k, 0)),
            ],
            scratch_shapes=[pltpu.VMEM((width, n_c), BF)],
        ),
        out_shape=[
            jax.ShapeDtypeStruct((n_k, rows, n_c), BF),
            jax.ShapeDtypeStruct((n_k, n_c), F32),
        ],
        cost_estimate=pl.CostEstimate(
            flops=2 * n_k * rows * width * n_c, bytes_accessed=12 << 20, transcendentals=0
        ),
        compiler_params=pltpu.CompilerParams(vmem_limit_bytes=40 << 20),
        name="inner_products",
    )(row, coupling, cases)


def force_kernel(airy_ref, inner_ref, out_ref, total):
    slabs, rows, n_c = inner_ref.shape
    step = pl.program_id(0)
    acc = jnp.zeros((rows, n_c), F32)
    for k in range(slabs):
        acc = acc + airy_ref[k : k + 1, :].astype(F32) * inner_ref[k].astype(F32)

    @pl.when(step == 0)
    def _():
        total[...] = acc

    @pl.when(step > 0)
    def _():
        total[...] += acc

    @pl.when(step == pl.num_programs(0) - 1)
    def _():
        for g in range(n_c // 32):
            out_ref[g] = jnp.concatenate(
                [total[8 * a : 8 * a + 8, 32 * g : 32 * g + 32] for a in range(4)], axis=1
            ).astype(out_ref.dtype)


def forces(airy, inner, slabs=32):
    n_k, rows, n_c = inner.shape
    return pl.pallas_call(
        force_kernel,
        grid=(n_k // slabs,),
        in_specs=[
            pl.BlockSpec((slabs, n_c), lambda k: (k, 0)),
            pl.BlockSpec((slabs, rows, n_c), lambda k: (k, 0, 0)),
        ],
        out_specs=pl.BlockSpec((n_c // 32, 8, 128), lambda k: (0, 0, 0)),
        out_shape=jax.ShapeDtypeStruct((n_c // 32, 8, 128), BF),
        scratch_shapes=[pltpu.VMEM((rows, n_c), F32)],
        cost_estimate=pl.CostEstimate(
            flops=2 * n_k * rows * n_c, bytes_accessed=4 << 20, transcendentals=0
        ),
        compiler_params=pltpu.CompilerParams(vmem_limit_bytes=32 << 20),
        name="forces",
    )(airy, inner)


def final_kernel(parts_ref, base_ref, damping_ref, out_ref):
    total = parts_ref[0].astype(F32)
    for i in range(1, parts_ref.shape[0]):
        total = total + parts_ref[i].astype(F32)
    spread = jnp.concatenate([total[:, :, 32 * a : 32 * a + 32] for a in range(4)], axis=1)
    force = spread.reshape(1024, 32).T
    out_ref[...] = (base_ref[...] - force) / (1.0 + damping_ref[...])


def final_step(parts, base, damping):
    return pl.pallas_call(
        final_kernel,
        out_shape=jax.ShapeDtypeStruct(base.shape, F32),
        compiler_params=pltpu.CompilerParams(vmem_limit_bytes=16 << 20),
        name="final_step",
    )(parts, base, damping)


def exchange(x, axes):
    return lax.all_to_all(x, axes, split_axis=0, concat_axis=0, tiled=True)


def spread(x, axes, n):
    return exchange(jnp.broadcast_to(x[None], (n, *x.shape)), axes)


def swap(x):
    return lax.ppermute(x, "c", [(0, 1), (1, 0)])


def shards(
    amplitudes, previous, coupling, stiffness, airy_scale, damping, strike_mode, strike_offset
):
    n_k, rows, width = coupling.shape
    core = lax.axis_index("c")
    inplane = lax.axis_index(INPLANE)
    same = lax.axis_index(SAME)
    row = lax.axis_index(ROW)
    depth = width // N_IN

    rounded = amplitudes.astype(BF)
    piece = lax.dynamic_slice_in_dim(rounded, inplane * depth, depth, 1)
    slab = spread(piece, SAME, N_SAME).reshape(N_SAME * rows, depth)
    own = spread(slab, INPLANE, N_IN)
    other = swap(own)

    index = row.astype(jnp.int32).reshape(1)
    inner_own, part_own = inner_products(index, coupling, own)
    inner_other, part_other = inner_products(index, coupling, other)

    part = part_own + swap(part_other.astype(BF)).astype(F32)
    per = n_k // N_SAME
    n_half = part.shape[1]
    shares = exchange(part.astype(BF).reshape(N_SAME, per, n_half), SAME)
    scale = lax.dynamic_slice_in_dim(airy_scale, same * per, per, 0)
    summed = jnp.sum(shares.astype(F32), axis=0) / scale[:, None]
    airy_own = spread(summed.astype(BF), SAME, N_SAME).reshape(n_k, n_half)
    airy_other = swap(airy_own)

    force_own = forces(airy_own, inner_own)
    force_other = forces(airy_other, inner_other)

    def by_core(mine, theirs):
        first = jnp.where(core == 0, mine, theirs)
        second = jnp.where(core == 0, theirs, mine)
        return jnp.stack([first, second], axis=1)

    messages = by_core(force_own, force_other).reshape(2 * N_SAME, 8, 128)
    arrived = exchange(messages, ROW)
    parts = spread(arrived, INPLANE, N_IN)

    offset = strike_offset.astype(F32)
    pulse = jnp.where(
        strike_offset <= STRIKE_LEN, 2.0 * (1.0 - jnp.cos(jnp.pi * offset / STRIKE_LEN)), 0.0
    )
    modes = jnp.arange(width, dtype=jnp.int32)
    excite = jnp.where(modes[None, :] == strike_mode[:, None], pulse[:, None], 0.0)
    base = 2.0 * amplitudes - (1.0 - damping) * previous - stiffness * amplitudes + excite
    result = final_step(parts, base, damping[None, :])

    airy = by_core(
        airy_own.T.reshape(N_SAME, rows, n_k), airy_other.T.reshape(N_SAME, rows, n_k)
    ).reshape(2 * N_SAME * rows, n_k)
    return (result, airy.astype(F32))


def solution(mesh):
    fine = Mesh(mesh.devices.reshape(SIZES), AXES)
    return jax.shard_map(
        shards,
        mesh=fine,
        in_specs=(
            P(ROW, None),
            P(ROW, None),
            P(INPLANE, ROW, None),
            P(),
            P(INPLANE),
            P(),
            P(ROW),
            P(ROW),
        ),
        out_specs=(P(ROW, None), P(None, INPLANE)),
        check_vma=False,
    )
```

```python
import functools

import jax
import jax.numpy as jnp
from jax import lax
from jax.experimental import pallas as pl
from jax.experimental.pallas import tpu as pltpu
from jax.sharding import Mesh, PartitionSpec as P

STRIKE_LEN = 64
AXES = ("xh", "y", "xl", "z", "c")
SIZES = (2, 4, 2, 8, 2)
INPLANE = ("xh", "y")
ROW = ("xl", "z", "c")
SAME = ("xl", "z")
N_IN = 8
N_Y = 4
N_SAME = 16
BF = jnp.bfloat16
F32 = jnp.float32


def inner_kernel(row_ref, tensor_ref, cases_ref, inner_ref, part_ref, turned):
    blocks, cases, depth = cases_ref.shape
    slabs, rows, width = tensor_ref.shape

    @pl.when(pl.program_id(0) == 0)
    def _():
        for i in range(blocks):
            turned[i * depth : (i + 1) * depth, :] = cases_ref[i].T

    start = pl.multiple_of(row_ref[0] * rows, rows)
    columns = turned[pl.ds(start, rows), :].astype(F32)
    inner = jnp.dot(
        tensor_ref[...].reshape(slabs * rows, width), turned[...], preferred_element_type=F32
    ).reshape(slabs, rows, cases)
    inner_ref[...] = inner.astype(BF)
    part_ref[...] = jnp.sum(inner * columns[None], axis=1)


def inner_products(row, coupling, cases, first=0, n_c=512, slabs=32):
    n_k, rows, width = coupling.shape
    blocks, _, depth = cases.shape
    at = first // n_c
    return pl.pallas_call(
        inner_kernel,
        grid_spec=pltpu.PrefetchScalarGridSpec(
            num_scalar_prefetch=1,
            grid=(n_k // slabs,),
            in_specs=[
                pl.BlockSpec((slabs, rows, width), lambda k, r: (k, 0, 0)),
                pl.BlockSpec((blocks, n_c, depth), lambda k, r: (0, at, 0)),
            ],
            out_specs=[
                pl.BlockSpec((slabs, rows, n_c), lambda k, r: (k, 0, 0)),
                pl.BlockSpec((slabs, n_c), lambda k, r: (k, 0)),
            ],
            scratch_shapes=[pltpu.VMEM((width, n_c), BF)],
        ),
        out_shape=[
            pltpu.HBM((n_k, rows, n_c), BF),
            jax.ShapeDtypeStruct((n_k, n_c), F32),
        ],
        cost_estimate=pl.CostEstimate(
            flops=2 * n_k * rows * width * n_c, bytes_accessed=12 << 20, transcendentals=0
        ),
        compiler_params=pltpu.CompilerParams(vmem_limit_bytes=20 << 20),
        name="inner_products",
    )(row, pltpu.with_memory_space_constraint(coupling, pltpu.HBM), cases)


def force_kernel(airy_ref, *refs):
    *inner_refs, out_ref, total = refs
    step = pl.program_id(0)
    first = 0
    for inner_ref in inner_refs:
        slabs, rows, n_c = inner_ref.shape
        acc = jnp.zeros((rows, n_c), F32)
        for k in range(slabs):
            weight = airy_ref[k : k + 1, first : first + n_c].astype(F32)
            acc = acc + weight * inner_ref[k].astype(F32)

        @pl.when(step == 0)
        def _():
            total[:, first : first + n_c] = acc

        @pl.when(step > 0)
        def _():
            total[:, first : first + n_c] += acc

        first += n_c

    @pl.when(step == pl.num_programs(0) - 1)
    def _():
        for g in range(first // 32):
            out_ref[g] = jnp.concatenate(
                [total[8 * a : 8 * a + 8, 32 * g : 32 * g + 32] for a in range(4)], axis=1
            ).astype(out_ref.dtype)


def forces(airy, inners, slabs=32):
    n_k, rows, _ = inners[0].shape
    n_c = airy.shape[1]
    return pl.pallas_call(
        force_kernel,
        grid=(n_k // slabs,),
        in_specs=[pl.BlockSpec((slabs, n_c), lambda k: (k, 0))]
        + [pl.BlockSpec((slabs, rows, i.shape[2]), lambda k: (k, 0, 0)) for i in inners],
        out_specs=pl.BlockSpec((n_c // 32, 8, 128), lambda k: (0, 0, 0)),
        out_shape=jax.ShapeDtypeStruct((n_c // 32, 8, 128), BF),
        scratch_shapes=[pltpu.VMEM((rows, n_c), F32)],
        cost_estimate=pl.CostEstimate(
            flops=2 * n_k * rows * n_c, bytes_accessed=4 << 20, transcendentals=0
        ),
        compiler_params=pltpu.CompilerParams(vmem_limit_bytes=12 << 20),
        name="forces",
    )(airy, *[pltpu.with_memory_space_constraint(i, pltpu.HBM) for i in inners])


def final_kernel(parts_ref, base_ref, damping_ref, out_ref):
    total = parts_ref[0].astype(F32)
    for i in range(1, parts_ref.shape[0]):
        total = total + parts_ref[i].astype(F32)
    spread = jnp.concatenate([total[:, :, 32 * a : 32 * a + 32] for a in range(4)], axis=1)
    force = spread.reshape(1024, 32).T
    out_ref[...] = (base_ref[...] - force) / (1.0 + damping_ref[...])


def final_step(parts, base, damping):
    return pl.pallas_call(
        final_kernel,
        out_shape=jax.ShapeDtypeStruct(base.shape, F32),
        compiler_params=pltpu.CompilerParams(vmem_limit_bytes=16 << 20),
        name="final_step",
    )(parts, base, damping)


def exchange(x, axes):
    return lax.all_to_all(x, axes, split_axis=0, concat_axis=0, tiled=True)


def spread(x, axes, n):
    return exchange(jnp.broadcast_to(x[None], (n, *x.shape)), axes)


def swap(x):
    return lax.ppermute(x, "c", [(0, 1), (1, 0)])


def shards(
    amplitudes, previous, coupling, stiffness, airy_scale, damping, strike_mode, strike_offset
):
    n_k, rows, width = coupling.shape
    core = lax.axis_index("c")
    same = lax.axis_index(SAME)
    row = lax.axis_index(ROW)
    depth = width // N_Y

    rounded = amplitudes.astype(BF)
    piece = lax.dynamic_slice_in_dim(rounded, lax.axis_index("y") * depth, depth, 1)
    slab = spread(piece, SAME, N_SAME).reshape(N_SAME * rows, depth)
    own = spread(slab, "y", N_Y)
    other = swap(own)

    index = row.astype(jnp.int32).reshape(1)
    inner_own_a, part_own_a = inner_products(index, coupling, own, 0, 256)
    other, part_own_a = lax.optimization_barrier((other, part_own_a))
    inner_other, part_other = inner_products(index, coupling, other)
    own, part_other = lax.optimization_barrier((own, part_other))
    inner_own_b, part_own_b = inner_products(index, coupling, own, 256, 256)

    part_own = jnp.concatenate([part_own_a, part_own_b], axis=1)
    part = part_own + swap(part_other.astype(BF)).astype(F32)
    per = n_k // N_SAME
    n_half = part.shape[1]
    shares = exchange(part.astype(BF).reshape(N_SAME, per, n_half), SAME)
    scale = lax.dynamic_slice_in_dim(airy_scale, same * per, per, 0)
    summed = jnp.sum(shares.astype(F32), axis=0) / scale[:, None]
    airy_own = spread(summed.astype(BF), SAME, N_SAME).reshape(n_k, n_half)
    airy_other = swap(airy_own)

    force_other = forces(airy_other, [inner_other])
    force_own = forces(airy_own, [inner_own_a, inner_own_b])

    def by_core(mine, theirs):
        first = jnp.where(core == 0, mine, theirs)
        second = jnp.where(core == 0, theirs, mine)
        return jnp.stack([first, second], axis=1)

    messages = by_core(force_own, swap(force_other))
    everywhere = jnp.broadcast_to(messages[None], (N_IN, *messages.shape))
    arrived = exchange(everywhere.reshape(N_IN * N_SAME, 16, 128), INPLANE + SAME)
    parts = arrived.reshape(N_IN, 2 * N_SAME, 8, 128)

    offset = strike_offset.astype(F32)
    pulse = jnp.where(
        strike_offset <= STRIKE_LEN, 2.0 * (1.0 - jnp.cos(jnp.pi * offset / STRIKE_LEN)), 0.0
    )
    modes = jnp.arange(width, dtype=jnp.int32)
    excite = jnp.where(modes[None, :] == strike_mode[:, None], pulse[:, None], 0.0)
    base = 2.0 * amplitudes - (1.0 - damping) * previous - stiffness * amplitudes + excite
    result = final_step(parts, base, damping[None, :])

    airy = by_core(
        airy_own.T.reshape(N_SAME, rows, n_k), airy_other.T.reshape(N_SAME, rows, n_k)
    ).reshape(2 * N_SAME * rows, n_k)
    return (result, airy.astype(F32))


def solution(mesh):
    fine = Mesh(mesh.devices.reshape(SIZES), AXES)
    return jax.shard_map(
        shards,
        mesh=fine,
        in_specs=(
            P(ROW, None),
            P(ROW, None),
            P(INPLANE, ROW, None),
            P(),
            P(INPLANE),
            P(),
            P(ROW),
            P(ROW),
        ),
        out_specs=(P(ROW, None), P(None, INPLANE)),
        check_vma=False,
    )
```

```python
import functools

import jax
import jax.numpy as jnp
from jax import lax
from jax.experimental import pallas as pl
from jax.experimental.pallas import tpu as pltpu
from jax.sharding import Mesh, PartitionSpec as P

STRIKE_LEN = 64
AXES = ("xh", "y", "xl", "z", "c")
SIZES = (2, 4, 2, 8, 2)
INPLANE = ("xh", "y")
ROW = ("xl", "z", "c")
SAME = ("xl", "z")
N_IN = 8
N_Y = 4
N_SAME = 16
WIDE = 128
BF = jnp.bfloat16
F32 = jnp.float32


def inner_kernel(counts, row_ref, tensor_ref, *refs):
    n_in, blocks = sum(counts), len(counts)
    case_refs = refs[:n_in]
    inner_refs = refs[n_in : n_in + blocks]
    part_refs = refs[n_in + blocks : n_in + 2 * blocks]
    turned = refs[-1]
    slabs, rows, width = tensor_ref.shape

    @pl.when(pl.program_id(0) == 0)
    def _():
        at = 0
        for b, count in enumerate(counts):
            pieces = [case_refs[at + i][...] for i in range(count)]
            whole = pieces[0] if count == 1 else jnp.concatenate(pieces, axis=0)
            turned[:, b * WIDE : (b + 1) * WIDE] = whole.T
            at += count

    start = pl.multiple_of(row_ref[0] * rows, rows)
    columns = turned[pl.ds(start, rows), :].astype(F32)
    inner = jnp.dot(
        tensor_ref[...].reshape(slabs * rows, width), turned[...], preferred_element_type=F32
    ).reshape(slabs, rows, blocks * WIDE)
    for b in range(blocks):
        span = slice(b * WIDE, (b + 1) * WIDE)
        piece = inner[:, :, span]
        inner_refs[b][...] = piece.astype(BF)
        part = jnp.sum(piece * columns[None, :, span], axis=1)
        part_refs[b][...] = part.astype(part_refs[b].dtype)


def inner_products(row, coupling, groups, part_types, slabs=32):
    n_k, rows, width = coupling.shape
    counts = tuple(len(g) for g in groups)
    cases = [c for g in groups for c in g]
    blocks = len(groups)
    out = pl.pallas_call(
        functools.partial(inner_kernel, counts),
        grid_spec=pltpu.PrefetchScalarGridSpec(
            num_scalar_prefetch=1,
            grid=(n_k // slabs,),
            in_specs=[pl.BlockSpec((slabs, rows, width), lambda k, r: (k, 0, 0))]
            + [pl.BlockSpec(c.shape, lambda k, r: (0, 0)) for c in cases],
            out_specs=[pl.BlockSpec((slabs, rows, WIDE), lambda k, r: (k, 0, 0))] * blocks
            + [pl.BlockSpec((slabs, WIDE), lambda k, r: (k, 0))] * blocks,
            scratch_shapes=[pltpu.VMEM((width, blocks * WIDE), BF)],
        ),
        out_shape=[pltpu.HBM((n_k, rows, WIDE), BF)] * blocks
        + [jax.ShapeDtypeStruct((n_k, WIDE), t) for t in part_types],
        cost_estimate=pl.CostEstimate(
            flops=2 * n_k * rows * width * blocks * WIDE, bytes_accessed=10 << 20, transcendentals=0
        ),
        compiler_params=pltpu.CompilerParams(vmem_limit_bytes=24 << 20),
        name="inner_products",
    )(row, coupling, *cases)
    return out[:blocks], out[blocks:]


def combine_kernel(*refs):
    *sources, out_ref = refs
    half = len(sources) // 2
    for b in range(half):
        total = sources[b][...] + sources[half + b][...].astype(F32)
        out_ref[:, b * WIDE : (b + 1) * WIDE] = total.astype(BF)


def combine(mine, received):
    n_k = mine[0].shape[0]
    return pl.pallas_call(
        combine_kernel,
        out_shape=jax.ShapeDtypeStruct((n_k, WIDE * len(mine)), BF),
        compiler_params=pltpu.CompilerParams(vmem_limit_bytes=4 << 20),
        name="combine",
    )(*mine, *received)


def force_kernel(pair, place_ref, airy_ref, *refs):
    if pair:
        *inner_refs, mine_ref, out_ref, total = refs
    else:
        *inner_refs, out_ref, total = refs
    step = pl.program_id(0)
    slabs, rows, _ = inner_refs[0].shape
    y, core = place_ref[0], place_ref[1]

    for d, inner_ref in enumerate(inner_refs):
        acc = jnp.zeros((rows, WIDE), F32)
        for k in range(slabs):
            weight = airy_ref[k : k + 1, d * WIDE : (d + 1) * WIDE].astype(F32)
            acc = acc + weight * inner_ref[k].astype(F32)
        at = pl.ds(pl.multiple_of(((y + d) % N_Y) * rows, rows), rows)

        @pl.when(step == 0)
        def _():
            total[at, :] = acc

        @pl.when(step > 0)
        def _():
            total[at, :] += acc

    @pl.when(step == pl.num_programs(0) - 1)
    def _():
        turned = total[...].T.astype(BF).reshape(N_SAME, 8, WIDE)
        if pair:
            out_ref[:, core] = mine_ref[...]
            out_ref[:, 1 - core] = turned
        else:
            out_ref[...] = turned


def forces(place, airy, inners, mine=None, slabs=32):
    n_k, rows, _ = inners[0].shape
    pair = mine is not None
    shape = (N_SAME, 2, 8, WIDE) if pair else (N_SAME, 8, WIDE)
    extra = [mine] if pair else []
    return pl.pallas_call(
        functools.partial(force_kernel, pair),
        grid_spec=pltpu.PrefetchScalarGridSpec(
            num_scalar_prefetch=1,
            grid=(n_k // slabs,),
            in_specs=[pl.BlockSpec((slabs, airy.shape[1]), lambda k, s: (k, 0))]
            + [pl.BlockSpec((slabs, rows, WIDE), lambda k, s: (k, 0, 0))] * len(inners)
            + [pl.BlockSpec(m.shape, lambda k, s: (0, 0, 0)) for m in extra],
            out_specs=pl.BlockSpec(shape, lambda k, s: (0,) * len(shape)),
            scratch_shapes=[pltpu.VMEM((N_Y * rows, WIDE), F32)],
        ),
        out_shape=jax.ShapeDtypeStruct(shape, BF),
        cost_estimate=pl.CostEstimate(
            flops=2 * n_k * rows * airy.shape[1], bytes_accessed=4 << 20, transcendentals=0
        ),
        compiler_params=pltpu.CompilerParams(vmem_limit_bytes=12 << 20),
        name="forces",
    )(place, airy, *[pltpu.with_memory_space_constraint(i, pltpu.HBM) for i in inners], *extra)


def airy_kernel(place_ref, mine_ref, theirs_ref, out_ref):
    y, core = place_ref[0], place_ref[1]
    for source, at in ((mine_ref, core), (theirs_ref, 1 - core)):
        for d in range(N_Y):
            piece = source[:, d * WIDE : (d + 1) * WIDE].astype(F32).T
            out_ref[:, at, (y + d) % N_Y] = piece.reshape(N_SAME, 8, WIDE)


def airy_output(place, mine, theirs):
    full = pl.BlockSpec(mine.shape, lambda i, s: (0, 0))
    shape = (N_SAME, 2, N_Y, 8, WIDE)
    return pl.pallas_call(
        airy_kernel,
        grid_spec=pltpu.PrefetchScalarGridSpec(
            num_scalar_prefetch=1,
            grid=(1,),
            in_specs=[full, full],
            out_specs=pl.BlockSpec(shape, lambda i, s: (0,) * 5),
        ),
        out_shape=jax.ShapeDtypeStruct(shape, F32),
        cost_estimate=pl.CostEstimate(flops=1 << 20, bytes_accessed=1 << 20, transcendentals=0),
        compiler_params=pltpu.CompilerParams(vmem_limit_bytes=8 << 20),
        name="airy_output",
    )(place, mine, theirs)


def final_kernel(parts_ref, base_ref, damping_ref, out_ref):
    total = parts_ref[0].astype(F32)
    for i in range(1, parts_ref.shape[0]):
        total = total + parts_ref[i].astype(F32)
    scale = 1.0 + damping_ref[...]
    for a in range(4):
        rows = slice(8 * a, 8 * a + 8)
        force = jnp.concatenate(
            [total[r][:, 32 * a : 32 * a + 32] for r in range(2 * N_SAME)], axis=1
        )
        out_ref[rows, :] = (base_ref[rows, :] - force) / scale


def final_step(parts, base, damping):
    return pl.pallas_call(
        final_kernel,
        out_shape=jax.ShapeDtypeStruct(base.shape, F32),
        compiler_params=pltpu.CompilerParams(vmem_limit_bytes=16 << 20),
        name="final_step",
    )(parts, base, damping)


def exchange(x, axes):
    return lax.all_to_all(x, axes, split_axis=0, concat_axis=0, tiled=True)


def spread(x, axes, n):
    return exchange(jnp.broadcast_to(x[None], (n, *x.shape)), axes)


def swap(x):
    return lax.ppermute(x, "c", [(0, 1), (1, 0)])


def shift(x, by):
    return lax.ppermute(x, "y", [(i, (i + by) % N_Y) for i in range(N_Y)])


def after(x):
    return lax.optimization_barrier(x)


def shards(
    amplitudes, previous, coupling, stiffness, airy_scale, damping, strike_mode, strike_offset
):
    n_k, rows, width = coupling.shape
    y = lax.axis_index("y").astype(jnp.int32)
    core = lax.axis_index("c").astype(jnp.int32)
    same = lax.axis_index(SAME)
    row = lax.axis_index(ROW).astype(jnp.int32).reshape(1)
    place = jnp.stack([y, core])
    few = rows // N_Y

    piece = lax.dynamic_slice_in_dim(amplitudes, y * few, few, 0).astype(BF)
    b0 = spread(piece, SAME, N_SAME).reshape(WIDE, width)
    b3, b1 = shift(b0, 1), shift(b0, -1)
    o0 = swap(b0)
    (i0, j0), (p0, q0) = inner_products(row, coupling, [[b0], [o0]], [F32, BF])

    b1, b3, p0, q0 = after((b1, b3, p0, q0))
    b2a, b2b = shift(b3[: WIDE // 2], 1), shift(b1[WIDE // 2 :], -1)
    o1, o3 = swap(b1), swap(b3)
    (i1, i3), (p1, p3) = inner_products(row, coupling, [[b1], [b3]], [F32, F32])

    o1, o3, b2a, b2b, p1 = after((o1, o3, b2a, b2b, p1))
    o2a, o2b = swap(b2a), swap(b2b)
    (j1, j3), (q1, q3) = inner_products(row, coupling, [[o1], [o3]], [BF, BF])

    b2a, b2b, o2a, o2b, q1 = after((b2a, b2b, o2a, o2b, q1))
    (i2, j2), (p2, q2) = inner_products(row, coupling, [[b2a, b2b], [o2a, o2b]], [F32, BF])

    received = [swap(q) for q in (q0, q1, q2, q3)]
    part = combine([p0, p1, p2, p3], received)
    per = n_k // N_SAME
    n_half = part.shape[1]
    shares = exchange(part.reshape(N_SAME, per, n_half), SAME)
    scale = lax.dynamic_slice_in_dim(airy_scale, same * per, per, 0)
    summed = jnp.sum(shares.astype(F32), axis=0) / scale[:, None]
    airy_own = spread(summed.astype(BF), SAME, N_SAME).reshape(n_k, n_half)
    airy_other = swap(airy_own)

    force_own = forces(place, airy_own, [i0, i1, i2, i3])
    messages = forces(place, airy_other, [j0, j1, j2, j3], force_own)
    arrived = exchange(messages.reshape(2 * N_SAME, 8, WIDE), ROW)
    parts = spread(arrived, INPLANE, N_IN)
    airy = airy_output(place, airy_own, airy_other).reshape(2 * N_SAME * rows, n_k)

    offset = strike_offset.astype(F32)
    pulse = jnp.where(
        strike_offset <= STRIKE_LEN, 2.0 * (1.0 - jnp.cos(jnp.pi * offset / STRIKE_LEN)), 0.0
    )
    modes = jnp.arange(width, dtype=jnp.int32)
    excite = jnp.where(modes[None, :] == strike_mode[:, None], pulse[:, None], 0.0)
    base = 2.0 * amplitudes - (1.0 - damping) * previous - stiffness * amplitudes + excite
    result = final_step(parts, base, damping[None, :])
    return (result, airy)


def solution(mesh):
    fine = Mesh(mesh.devices.reshape(SIZES), AXES)
    return jax.shard_map(
        shards,
        mesh=fine,
        in_specs=(
            P(ROW, None),
            P(ROW, None),
            P(INPLANE, ROW, None),
            P(),
            P(INPLANE),
            P(),
            P(ROW),
            P(ROW),
        ),
        out_specs=(P(ROW, None), P(None, INPLANE)),
        check_vma=False,
    )
```

```python
import functools

import jax
import jax.numpy as jnp
from jax import lax
from jax.experimental import pallas as pl
from jax.experimental.pallas import tpu as pltpu
from jax.sharding import Mesh, PartitionSpec as P

STRIKE_LEN = 64
AXES = ("xh", "y", "xl", "z", "c")
SIZES = (2, 4, 2, 8, 2)
INPLANE = ("xh", "y")
ROW = ("xl", "z", "c")
SAME = ("xl", "z")
N_IN = 8
N_Y = 4
N_SAME = 16
PARTS = 2
FEW = 16
WIDE = 256
BF = jnp.bfloat16
F32 = jnp.float32


def inner_kernel(counts, row_ref, tensor_ref, *refs):
    n_in, blocks = sum(counts), len(counts)
    case_refs = refs[:n_in]
    inner_refs = refs[n_in : n_in + blocks]
    part_refs = refs[n_in + blocks : n_in + 2 * blocks]
    turned = refs[-1]
    slabs, rows, width = tensor_ref.shape

    @pl.when(pl.program_id(0) == 0)
    def _():
        at = 0
        for b, count in enumerate(counts):
            pieces = [case_refs[at + i][...] for i in range(count)]
            whole = pieces[0] if count == 1 else jnp.concatenate(pieces, axis=0)
            turned[:, b * WIDE : (b + 1) * WIDE] = whole.T
            at += count

    start = pl.multiple_of(row_ref[0] * rows, rows)
    columns = turned[pl.ds(start, rows), :].astype(F32)
    inner = jnp.dot(
        tensor_ref[...].reshape(slabs * rows, width), turned[...], preferred_element_type=F32
    ).reshape(slabs, rows, blocks * WIDE)
    for b in range(blocks):
        span = slice(b * WIDE, (b + 1) * WIDE)
        piece = inner[:, :, span]
        inner_refs[b][...] = piece.astype(BF)
        part = jnp.sum(piece * columns[None, :, span], axis=1)
        part_refs[b][...] = part.astype(part_refs[b].dtype)


def inner_products(row, coupling, groups, part_types, slabs=32):
    n_k, rows, width = coupling.shape
    counts = tuple(len(g) for g in groups)
    cases = [c for g in groups for c in g]
    blocks = len(groups)
    out = pl.pallas_call(
        functools.partial(inner_kernel, counts),
        grid_spec=pltpu.PrefetchScalarGridSpec(
            num_scalar_prefetch=1,
            grid=(n_k // slabs,),
            in_specs=[pl.BlockSpec((slabs, rows, width), lambda k, r: (k, 0, 0))]
            + [pl.BlockSpec(c.shape, lambda k, r: (0, 0)) for c in cases],
            out_specs=[pl.BlockSpec((slabs, rows, WIDE), lambda k, r: (k, 0, 0))] * blocks
            + [pl.BlockSpec((slabs, WIDE), lambda k, r: (k, 0))] * blocks,
            scratch_shapes=[pltpu.VMEM((width, blocks * WIDE), BF)],
        ),
        out_shape=[pltpu.HBM((n_k, rows, WIDE), BF)] * blocks
        + [jax.ShapeDtypeStruct((n_k, WIDE), t) for t in part_types],
        cost_estimate=pl.CostEstimate(
            flops=2 * n_k * rows * width * blocks * WIDE, bytes_accessed=10 << 20, transcendentals=0
        ),
        compiler_params=pltpu.CompilerParams(vmem_limit_bytes=24 << 20),
        name="inner_products",
    )(row, coupling, *cases)
    return out[:blocks], out[blocks:]


def combine_kernel(*refs):
    *sources, out_ref = refs
    half = len(sources) // 2
    for b in range(half):
        total = sources[b][...] + sources[half + b][...].astype(F32)
        out_ref[:, b * WIDE : (b + 1) * WIDE] = total.astype(BF)


def combine(mine, received):
    n_k = mine[0].shape[0]
    return pl.pallas_call(
        combine_kernel,
        out_shape=jax.ShapeDtypeStruct((n_k, WIDE * len(mine)), BF),
        compiler_params=pltpu.CompilerParams(vmem_limit_bytes=4 << 20),
        name="combine",
    )(*mine, *received)


def force_kernel(pair, place_ref, airy_ref, *refs):
    if pair:
        *inner_refs, mine_ref, out_ref, total = refs
    else:
        *inner_refs, out_ref, total = refs
    step = pl.program_id(0)
    slabs, rows, _ = inner_refs[0].shape
    half, core = place_ref[0], place_ref[1]

    for d, inner_ref in enumerate(inner_refs):
        acc = jnp.zeros((rows, WIDE), F32)
        for k in range(slabs):
            weight = airy_ref[k : k + 1, d * WIDE : (d + 1) * WIDE].astype(F32)
            acc = acc + weight * inner_ref[k].astype(F32)
        at = pl.ds(pl.multiple_of(((half + d) % PARTS) * rows, rows), rows)

        @pl.when(step == 0)
        def _():
            total[at, :] = acc

        @pl.when(step > 0)
        def _():
            total[at, :] += acc

    @pl.when(step == pl.num_programs(0) - 1)
    def _():
        turned = total[...].T.reshape(N_SAME, FEW, PARTS * rows)
        turned = jnp.concatenate([turned[:, :8], turned[:, 8:]], axis=2).astype(BF)
        if pair:
            out_ref[:, core] = mine_ref[...]
            out_ref[:, 1 - core] = turned
        else:
            out_ref[...] = turned


def forces(place, airy, inners, mine=None, slabs=32):
    n_k, rows, _ = inners[0].shape
    pair = mine is not None
    shape = (N_SAME, 2, 8, 128) if pair else (N_SAME, 8, 128)
    extra = [mine] if pair else []
    return pl.pallas_call(
        functools.partial(force_kernel, pair),
        grid_spec=pltpu.PrefetchScalarGridSpec(
            num_scalar_prefetch=1,
            grid=(n_k // slabs,),
            in_specs=[pl.BlockSpec((slabs, airy.shape[1]), lambda k, s: (k, 0))]
            + [pl.BlockSpec((slabs, rows, WIDE), lambda k, s: (k, 0, 0))] * len(inners)
            + [pl.BlockSpec(m.shape, lambda k, s: (0, 0, 0)) for m in extra],
            out_specs=pl.BlockSpec(shape, lambda k, s: (0,) * len(shape)),
            scratch_shapes=[pltpu.VMEM((PARTS * rows, WIDE), F32)],
        ),
        out_shape=jax.ShapeDtypeStruct(shape, BF),
        cost_estimate=pl.CostEstimate(
            flops=2 * n_k * rows * airy.shape[1], bytes_accessed=4 << 20, transcendentals=0
        ),
        compiler_params=pltpu.CompilerParams(vmem_limit_bytes=12 << 20),
        name="forces",
    )(place, airy, *inners, *extra)


def airy_kernel(place_ref, mine_ref, theirs_ref, out_ref):
    half, core = place_ref[0], place_ref[1]
    for source, at in ((mine_ref, core), (theirs_ref, 1 - core)):
        for d in range(PARTS):
            piece = source[:, d * WIDE : (d + 1) * WIDE].astype(F32).T
            out_ref[:, at, (half + d) % PARTS] = piece.reshape(N_SAME, FEW, piece.shape[1])


def airy_output(place, mine, theirs):
    full = pl.BlockSpec(mine.shape, lambda i, s: (0, 0))
    shape = (N_SAME, 2, PARTS, FEW, mine.shape[0])
    return pl.pallas_call(
        airy_kernel,
        grid_spec=pltpu.PrefetchScalarGridSpec(
            num_scalar_prefetch=1,
            grid=(1,),
            in_specs=[full, full],
            out_specs=pl.BlockSpec(shape, lambda i, s: (0,) * 5),
        ),
        out_shape=jax.ShapeDtypeStruct(shape, F32),
        cost_estimate=pl.CostEstimate(flops=1 << 20, bytes_accessed=1 << 20, transcendentals=0),
        compiler_params=pltpu.CompilerParams(vmem_limit_bytes=8 << 20),
        name="airy_output",
    )(place, mine, theirs)


def final_kernel(parts_ref, base_ref, damping_ref, out_ref):
    total = parts_ref[0].astype(F32)
    for i in range(1, parts_ref.shape[0]):
        total = total + parts_ref[i].astype(F32)
    scale = 1.0 + damping_ref[...]
    for a in range(4):
        rows = slice(8 * a, 8 * a + 8)
        at = (a % 2) * 64 + (a // 2) * 32
        force = jnp.concatenate([total[r][:, at : at + 32] for r in range(2 * N_SAME)], axis=1)
        out_ref[rows, :] = (base_ref[rows, :] - force) / scale


def final_step(parts, base, damping):
    return pl.pallas_call(
        final_kernel,
        out_shape=jax.ShapeDtypeStruct(base.shape, F32),
        compiler_params=pltpu.CompilerParams(vmem_limit_bytes=16 << 20),
        name="final_step",
    )(parts, base, damping)


def exchange(x, axes):
    return lax.all_to_all(x, axes, split_axis=0, concat_axis=0, tiled=True)


def spread(x, axes, n):
    return exchange(jnp.broadcast_to(x[None], (n, *x.shape)), axes)


def swap(x):
    return lax.ppermute(x, "c", [(0, 1), (1, 0)])


def shift(x, by):
    return lax.ppermute(x, "y", [(i, (i + by) % N_Y) for i in range(N_Y)])


def after(x):
    return lax.optimization_barrier(x)


def shards(
    amplitudes, previous, coupling, stiffness, airy_scale, damping, strike_mode, strike_offset
):
    n_k, rows, width = coupling.shape
    y = lax.axis_index("y").astype(jnp.int32)
    core = lax.axis_index("c").astype(jnp.int32)
    same = lax.axis_index(SAME)
    row = lax.axis_index(ROW).astype(jnp.int32).reshape(1)
    half = y % PARTS
    place = jnp.stack([half, core])

    piece = lax.dynamic_slice_in_dim(amplitudes, half * FEW, FEW, 0).astype(BF)
    b0 = spread(piece, SAME, N_SAME).reshape(WIDE, width)
    b1 = [shift(b0[: WIDE // 2], -1), shift(b0[WIDE // 2 :], 1)]
    o0 = swap(b0)
    (i0, j0), (p0, q0) = inner_products(row, coupling, [[b0], [o0]], [F32, BF])

    b1, p0, q0 = after((b1, p0, q0))
    o1 = [swap(b) for b in b1]
    (i1,), (p1,) = inner_products(row, coupling, [b1], [F32])

    o1, p1 = after((o1, p1))
    (j1,), (q1,) = inner_products(row, coupling, [o1], [BF])

    part = combine([p0, p1], [swap(q0), swap(q1)])
    per = n_k // N_SAME
    n_half = part.shape[1]
    shares = exchange(part.reshape(N_SAME, per, n_half), SAME)
    scale = lax.dynamic_slice_in_dim(airy_scale, same * per, per, 0)
    summed = jnp.sum(shares.astype(F32), axis=0) / scale[:, None]
    airy_own = spread(summed.astype(BF), SAME, N_SAME).reshape(n_k, n_half)
    airy_other = swap(airy_own)

    force_own = forces(place, airy_own, [i0, i1])
    messages = forces(place, airy_other, [j0, j1], force_own)
    arrived = exchange(messages.reshape(2 * N_SAME, 8, 128), ROW)
    parts = spread(arrived, INPLANE, N_IN)
    airy = airy_output(place, airy_own, airy_other).reshape(2 * N_SAME * rows, n_k)

    offset = strike_offset.astype(F32)
    pulse = jnp.where(
        strike_offset <= STRIKE_LEN, 2.0 * (1.0 - jnp.cos(jnp.pi * offset / STRIKE_LEN)), 0.0
    )
    modes = jnp.arange(width, dtype=jnp.int32)
    excite = jnp.where(modes[None, :] == strike_mode[:, None], pulse[:, None], 0.0)
    base = 2.0 * amplitudes - (1.0 - damping) * previous - stiffness * amplitudes + excite
    result = final_step(parts, base, damping[None, :])
    return (result, airy)


def solution(mesh):
    fine = Mesh(mesh.devices.reshape(SIZES), AXES)
    return jax.shard_map(
        shards,
        mesh=fine,
        in_specs=(
            P(ROW, None),
            P(ROW, None),
            P(INPLANE, ROW, None),
            P(),
            P(INPLANE),
            P(),
            P(ROW),
            P(ROW),
        ),
        out_specs=(P(ROW, None), P(None, INPLANE)),
        check_vma=False,
    )
```

```python
import functools

import jax
import jax.numpy as jnp
from jax import lax
from jax.experimental import pallas as pl
from jax.experimental.pallas import tpu as pltpu
from jax.sharding import Mesh, PartitionSpec as P

STRIKE_LEN = 64
AXES = ("xh", "y", "xl", "z", "c")
SIZES = (2, 4, 2, 8, 2)
INPLANE = ("xh", "y")
ROW = ("xl", "z", "c")
SAME = ("xl", "z")
N_IN = 8
N_Y = 4
N_SAME = 16
PARTS = 2
FEW = 16
WIDE = 256
BF = jnp.bfloat16
F32 = jnp.float32


VMEM = pl.BlockSpec(memory_space=pltpu.VMEM)


def in_vmem(x):
    return pltpu.with_memory_space_constraint(x, pltpu.VMEM)


def inner_kernel(counts, slabs, row_ref, tensor_ref, *refs):
    n_in, blocks = sum(counts), len(counts)
    case_refs = refs[:n_in]
    inner_refs = refs[n_in : n_in + blocks]
    part_refs = refs[n_in + blocks : n_in + 2 * blocks]
    turned = refs[-1]
    _, rows, width = tensor_ref.shape
    step = pl.program_id(0)

    @pl.when(step == 0)
    def _():
        at = 0
        for b, count in enumerate(counts):
            pieces = [case_refs[at + i][...] for i in range(count)]
            whole = pieces[0] if count == 1 else jnp.concatenate(pieces, axis=0)
            turned[:, b * WIDE : (b + 1) * WIDE] = whole.T
            at += count

    start = pl.multiple_of(row_ref[0] * rows, rows)
    columns = turned[pl.ds(start, rows), :].astype(F32)
    tensor = tensor_ref[pl.ds(step * slabs, slabs)]
    inner = jnp.dot(
        tensor.reshape(slabs * rows, width), turned[...], preferred_element_type=F32
    ).reshape(slabs, rows, blocks * WIDE)
    for b in range(blocks):
        span = slice(b * WIDE, (b + 1) * WIDE)
        piece = inner[:, :, span]
        inner_refs[b][...] = piece.astype(BF)
        part = jnp.sum(piece * columns[None, :, span], axis=1)
        part_refs[b][...] = part.astype(part_refs[b].dtype)


def inner_products(row, coupling, groups, part_types, slabs=32):
    n_k, rows, width = coupling.shape
    counts = tuple(len(g) for g in groups)
    cases = [c for g in groups for c in g]
    blocks = len(groups)
    out = pl.pallas_call(
        functools.partial(inner_kernel, counts, slabs),
        grid_spec=pltpu.PrefetchScalarGridSpec(
            num_scalar_prefetch=1,
            grid=(n_k // slabs,),
            in_specs=[VMEM] * (1 + len(cases)),
            out_specs=[pl.BlockSpec((slabs, rows, WIDE), lambda k, r: (k, 0, 0))] * blocks
            + [pl.BlockSpec((slabs, WIDE), lambda k, r: (k, 0))] * blocks,
            scratch_shapes=[pltpu.VMEM((width, blocks * WIDE), BF)],
        ),
        out_shape=[pltpu.HBM((n_k, rows, WIDE), BF)] * blocks
        + [jax.ShapeDtypeStruct((n_k, WIDE), t) for t in part_types],
        cost_estimate=pl.CostEstimate(
            flops=2 * n_k * rows * width * blocks * WIDE, bytes_accessed=10 << 20, transcendentals=0
        ),
        compiler_params=pltpu.CompilerParams(vmem_limit_bytes=20 << 20),
        name="inner_products",
    )(row, in_vmem(coupling), *[in_vmem(c) for c in cases])
    return out[:blocks], out[blocks:]


def combine_kernel(*refs):
    *sources, out_ref = refs
    half = len(sources) // 2
    for b in range(half):
        total = sources[b][...] + sources[half + b][...].astype(F32)
        out_ref[:, b * WIDE : (b + 1) * WIDE] = total.astype(BF)


def combine(mine, received):
    n_k = mine[0].shape[0]
    return pl.pallas_call(
        combine_kernel,
        out_shape=jax.ShapeDtypeStruct((n_k, WIDE * len(mine)), BF),
        compiler_params=pltpu.CompilerParams(vmem_limit_bytes=4 << 20),
        name="combine",
    )(*mine, *received)


def force_kernel(pair, place_ref, airy_ref, *refs):
    if pair:
        *inner_refs, mine_ref, out_ref, total = refs
    else:
        *inner_refs, out_ref, total = refs
    n_k, rows, _ = inner_refs[0].shape
    half, core = place_ref[0], place_ref[1]

    for d, inner_ref in enumerate(inner_refs):
        acc = jnp.zeros((rows, WIDE), F32)
        for k in range(n_k):
            weight = airy_ref[k : k + 1, d * WIDE : (d + 1) * WIDE].astype(F32)
            acc = acc + weight * inner_ref[k].astype(F32)
        at = pl.ds(pl.multiple_of(((half + d) % PARTS) * rows, rows), rows)
        total[at, :] = acc

    turned = total[...].T.reshape(N_SAME, FEW, PARTS * rows)
    turned = jnp.concatenate([turned[:, :8], turned[:, 8:]], axis=2).astype(BF)
    if pair:
        out_ref[:, core] = mine_ref[...]
        out_ref[:, 1 - core] = turned
    else:
        out_ref[...] = turned


def forces(place, airy, inners, mine=None):
    n_k, rows, _ = inners[0].shape
    pair = mine is not None
    shape = (N_SAME, 2, 8, 128) if pair else (N_SAME, 8, 128)
    operands = [airy, *inners] + ([mine] if pair else [])
    return pl.pallas_call(
        functools.partial(force_kernel, pair),
        in_specs=[pl.BlockSpec(memory_space=pltpu.SMEM)] + [VMEM] * len(operands),
        out_specs=VMEM,
        out_shape=jax.ShapeDtypeStruct(shape, BF),
        scratch_shapes=[pltpu.VMEM((PARTS * rows, WIDE), F32)],
        cost_estimate=pl.CostEstimate(
            flops=2 * n_k * rows * airy.shape[1], bytes_accessed=4 << 20, transcendentals=0
        ),
        compiler_params=pltpu.CompilerParams(vmem_limit_bytes=8 << 20),
        name="forces",
    )(place, *[in_vmem(x) for x in operands])


def airy_kernel(place_ref, mine_ref, theirs_ref, out_ref):
    half, core = place_ref[0], place_ref[1]
    for source, at in ((mine_ref, core), (theirs_ref, 1 - core)):
        for d in range(PARTS):
            piece = source[:, d * WIDE : (d + 1) * WIDE].astype(F32).T
            out_ref[:, at, (half + d) % PARTS] = piece.reshape(N_SAME, FEW, piece.shape[1])


def airy_output(place, mine, theirs):
    full = pl.BlockSpec(mine.shape, lambda i, s: (0, 0))
    shape = (N_SAME, 2, PARTS, FEW, mine.shape[0])
    return pl.pallas_call(
        airy_kernel,
        grid_spec=pltpu.PrefetchScalarGridSpec(
            num_scalar_prefetch=1,
            grid=(1,),
            in_specs=[full, full],
            out_specs=pl.BlockSpec(shape, lambda i, s: (0,) * 5),
        ),
        out_shape=jax.ShapeDtypeStruct(shape, F32),
        cost_estimate=pl.CostEstimate(flops=1 << 20, bytes_accessed=1 << 20, transcendentals=0),
        compiler_params=pltpu.CompilerParams(vmem_limit_bytes=8 << 20),
        name="airy_output",
    )(place, mine, theirs)


def final_kernel(parts_ref, base_ref, damping_ref, out_ref):
    total = parts_ref[0].astype(F32)
    for i in range(1, parts_ref.shape[0]):
        total = total + parts_ref[i].astype(F32)
    scale = 1.0 + damping_ref[...]
    for a in range(4):
        rows = slice(8 * a, 8 * a + 8)
        at = (a % 2) * 64 + (a // 2) * 32
        force = jnp.concatenate([total[r][:, at : at + 32] for r in range(2 * N_SAME)], axis=1)
        out_ref[rows, :] = (base_ref[rows, :] - force) / scale


def final_step(parts, base, damping):
    return pl.pallas_call(
        final_kernel,
        out_shape=jax.ShapeDtypeStruct(base.shape, F32),
        compiler_params=pltpu.CompilerParams(vmem_limit_bytes=16 << 20),
        name="final_step",
    )(parts, base, damping)


def exchange(x, axes):
    return lax.all_to_all(x, axes, split_axis=0, concat_axis=0, tiled=True)


def spread(x, axes, n):
    return exchange(jnp.broadcast_to(x[None], (n, *x.shape)), axes)


def swap(x):
    return lax.ppermute(x, "c", [(0, 1), (1, 0)])


def shift(x, by):
    return lax.ppermute(x, "y", [(i, (i + by) % N_Y) for i in range(N_Y)])


def after(x):
    return lax.optimization_barrier(x)


def shards(
    amplitudes, previous, coupling, stiffness, airy_scale, damping, strike_mode, strike_offset
):
    n_k, rows, width = coupling.shape
    y = lax.axis_index("y").astype(jnp.int32)
    core = lax.axis_index("c").astype(jnp.int32)
    same = lax.axis_index(SAME)
    row = lax.axis_index(ROW).astype(jnp.int32).reshape(1)
    half = y % PARTS
    place = jnp.stack([half, core])

    piece = lax.dynamic_slice_in_dim(amplitudes, half * FEW, FEW, 0).astype(BF)
    b0 = spread(piece, SAME, N_SAME).reshape(WIDE, width)
    b1 = [shift(b0[: WIDE // 2], -1), shift(b0[WIDE // 2 :], 1)]
    o0 = swap(b0)
    (i0, j0), (p0, q0) = inner_products(row, coupling, [[b0], [o0]], [F32, BF])

    b1, p0, q0 = after((b1, p0, q0))
    o1 = [swap(b) for b in b1]
    (i1,), (p1,) = inner_products(row, coupling, [b1], [F32])

    o1, p1 = after((o1, p1))
    (j1,), (q1,) = inner_products(row, coupling, [o1], [BF])

    part = combine([p0, p1], [swap(q0), swap(q1)])
    per = n_k // N_SAME
    n_half = part.shape[1]
    shares = exchange(part.reshape(N_SAME, per, n_half), SAME)
    scale = lax.dynamic_slice_in_dim(airy_scale, same * per, per, 0)
    summed = jnp.sum(shares.astype(F32), axis=0) / scale[:, None]
    airy_own = spread(summed.astype(BF), SAME, N_SAME).reshape(n_k, n_half)
    airy_other = swap(airy_own)

    force_own = forces(place, airy_own, [i0, i1])
    messages = forces(place, airy_other, [j0, j1], force_own)
    arrived = exchange(messages.reshape(2 * N_SAME, 8, 128), ROW)
    parts = spread(arrived, INPLANE, N_IN)
    airy = airy_output(place, airy_own, airy_other).reshape(2 * N_SAME * rows, n_k)

    offset = strike_offset.astype(F32)
    pulse = jnp.where(
        strike_offset <= STRIKE_LEN, 2.0 * (1.0 - jnp.cos(jnp.pi * offset / STRIKE_LEN)), 0.0
    )
    modes = jnp.arange(width, dtype=jnp.int32)
    excite = jnp.where(modes[None, :] == strike_mode[:, None], pulse[:, None], 0.0)
    base = 2.0 * amplitudes - (1.0 - damping) * previous - stiffness * amplitudes + excite
    result = final_step(parts, base, damping[None, :])
    return (result, airy)


def solution(mesh):
    fine = Mesh(mesh.devices.reshape(SIZES), AXES)
    return jax.shard_map(
        shards,
        mesh=fine,
        in_specs=(
            P(ROW, None),
            P(ROW, None),
            P(INPLANE, ROW, None),
            P(),
            P(INPLANE),
            P(),
            P(ROW),
            P(ROW),
        ),
        out_specs=(P(ROW, None), P(None, INPLANE)),
        check_vma=False,
    )
```

```python
import functools

import jax
import jax.numpy as jnp
from jax import lax
from jax.experimental import pallas as pl
from jax.experimental.pallas import tpu as pltpu
from jax.sharding import Mesh, PartitionSpec as P

STRIKE_LEN = 64
AXES = ("xh", "y", "xl", "z", "c")
SIZES = (2, 4, 2, 8, 2)
INPLANE = ("xh", "y")
ROW = ("xl", "z", "c")
SAME = ("xl", "z")
N_IN = 8
N_Y = 4
N_SAME = 16
PARTS = 2
FEW = 16
WIDE = 256
BF = jnp.bfloat16
F32 = jnp.float32


VMEM = pl.BlockSpec(memory_space=pltpu.VMEM)


def in_vmem(x):
    return pltpu.with_memory_space_constraint(x, pltpu.VMEM)


def inner_kernel(counts, slabs, stream, row_ref, tensor_ref, *refs):
    n_in, blocks = sum(counts), len(counts)
    case_refs = refs[:n_in]
    inner_refs = refs[n_in : n_in + blocks]
    part_refs = refs[n_in + blocks : n_in + 2 * blocks]
    turned = refs[-1]
    _, rows, width = tensor_ref.shape
    step = pl.program_id(0)

    @pl.when(step == 0)
    def _():
        at = 0
        for b, count in enumerate(counts):
            pieces = [case_refs[at + i][...] for i in range(count)]
            whole = pieces[0] if count == 1 else jnp.concatenate(pieces, axis=0)
            turned[:, b * WIDE : (b + 1) * WIDE] = whole.T
            at += count

    start = pl.multiple_of(row_ref[0] * rows, rows)
    columns = turned[pl.ds(start, rows), :].astype(F32)
    tensor = tensor_ref[...] if stream else tensor_ref[pl.ds(step * slabs, slabs)]
    inner = jnp.dot(
        tensor.reshape(slabs * rows, width), turned[...], preferred_element_type=F32
    ).reshape(slabs, rows, blocks * WIDE)
    for b in range(blocks):
        span = slice(b * WIDE, (b + 1) * WIDE)
        piece = inner[:, :, span]
        inner_refs[b][...] = piece.astype(BF)
        part = jnp.sum(piece * columns[None, :, span], axis=1)
        at = pl.ds(pl.multiple_of(step * slabs, slabs), slabs)
        part_refs[b][at, :] = part.astype(part_refs[b].dtype)


def inner_products(row, coupling, groups, part_types, slabs=32, stream=False):
    n_k, rows, width = coupling.shape
    counts = tuple(len(g) for g in groups)
    cases = [c for g in groups for c in g]
    blocks = len(groups)
    placed = pltpu.with_memory_space_constraint(coupling, pltpu.HBM if stream else pltpu.VMEM)
    out = pl.pallas_call(
        functools.partial(inner_kernel, counts, slabs, stream),
        grid_spec=pltpu.PrefetchScalarGridSpec(
            num_scalar_prefetch=1,
            grid=(n_k // slabs,),
            in_specs=[pl.BlockSpec((slabs, rows, width), lambda k, r: (k, 0, 0)) if stream else VMEM]
            + [VMEM] * len(cases),
            out_specs=[pl.BlockSpec((slabs, rows, WIDE), lambda k, r: (k, 0, 0))] * blocks
            + [VMEM] * blocks,
            scratch_shapes=[pltpu.VMEM((width, blocks * WIDE), BF)],
        ),
        out_shape=[pltpu.HBM((n_k, rows, WIDE), BF)] * blocks
        + [jax.ShapeDtypeStruct((n_k, WIDE), t) for t in part_types],
        cost_estimate=pl.CostEstimate(
            flops=2 * n_k * rows * width * blocks * WIDE, bytes_accessed=10 << 20, transcendentals=0
        ),
        compiler_params=pltpu.CompilerParams(vmem_limit_bytes=20 << 20),
        name="inner_products",
    )(row, placed, *[in_vmem(c) for c in cases])
    return out[:blocks], out[blocks:]


def combine_kernel(*refs):
    *sources, out_ref = refs
    half = len(sources) // 2
    for b in range(half):
        total = sources[b][...] + sources[half + b][...].astype(F32)
        out_ref[:, b * WIDE : (b + 1) * WIDE] = total.astype(BF)


def combine(mine, received):
    n_k = mine[0].shape[0]
    return pl.pallas_call(
        combine_kernel,
        out_shape=jax.ShapeDtypeStruct((n_k, WIDE * len(mine)), BF),
        compiler_params=pltpu.CompilerParams(vmem_limit_bytes=4 << 20),
        name="combine",
    )(*mine, *received)


def force_kernel(pair, place_ref, airy_ref, *refs):
    if pair:
        *inner_refs, mine_ref, out_ref, total = refs
    else:
        *inner_refs, out_ref, total = refs
    n_k, rows, _ = inner_refs[0].shape
    half, core = place_ref[0], place_ref[1]

    for d, inner_ref in enumerate(inner_refs):
        acc = jnp.zeros((rows, WIDE), F32)
        for k in range(n_k):
            weight = airy_ref[k : k + 1, d * WIDE : (d + 1) * WIDE].astype(F32)
            acc = acc + weight * inner_ref[k].astype(F32)
        at = pl.ds(pl.multiple_of(((half + d) % PARTS) * rows, rows), rows)
        total[at, :] = acc

    turned = total[...].T.reshape(N_SAME, FEW, PARTS * rows)
    turned = jnp.concatenate([turned[:, :8], turned[:, 8:]], axis=2).astype(BF)
    if pair:
        out_ref[:, core] = mine_ref[...]
        out_ref[:, 1 - core] = turned
    else:
        out_ref[...] = turned


def forces(place, airy, inners, mine=None):
    n_k, rows, _ = inners[0].shape
    pair = mine is not None
    shape = (N_SAME, 2, 8, 128) if pair else (N_SAME, 8, 128)
    operands = [airy, *inners] + ([mine] if pair else [])
    return pl.pallas_call(
        functools.partial(force_kernel, pair),
        in_specs=[pl.BlockSpec(memory_space=pltpu.SMEM)] + [VMEM] * len(operands),
        out_specs=VMEM,
        out_shape=jax.ShapeDtypeStruct(shape, BF),
        scratch_shapes=[pltpu.VMEM((PARTS * rows, WIDE), F32)],
        cost_estimate=pl.CostEstimate(
            flops=2 * n_k * rows * airy.shape[1], bytes_accessed=4 << 20, transcendentals=0
        ),
        compiler_params=pltpu.CompilerParams(vmem_limit_bytes=8 << 20),
        name="forces",
    )(place, *[in_vmem(x) for x in operands])


def airy_kernel(place_ref, mine_ref, theirs_ref, out_ref):
    half, core = place_ref[0], place_ref[1]
    for source, at in ((mine_ref, core), (theirs_ref, 1 - core)):
        for d in range(PARTS):
            piece = source[:, d * WIDE : (d + 1) * WIDE].astype(F32).T
            out_ref[:, at, (half + d) % PARTS] = piece.reshape(N_SAME, FEW, piece.shape[1])


def airy_output(place, mine, theirs):
    full = pl.BlockSpec(mine.shape, lambda i, s: (0, 0))
    shape = (N_SAME, 2, PARTS, FEW, mine.shape[0])
    return pl.pallas_call(
        airy_kernel,
        grid_spec=pltpu.PrefetchScalarGridSpec(
            num_scalar_prefetch=1,
            grid=(1,),
            in_specs=[full, full],
            out_specs=pl.BlockSpec(shape, lambda i, s: (0,) * 5),
        ),
        out_shape=jax.ShapeDtypeStruct(shape, F32),
        cost_estimate=pl.CostEstimate(flops=1 << 20, bytes_accessed=1 << 20, transcendentals=0),
        compiler_params=pltpu.CompilerParams(vmem_limit_bytes=8 << 20),
        name="airy_output",
    )(place, mine, theirs)


def final_kernel(parts_ref, base_ref, damping_ref, out_ref):
    total = parts_ref[0].astype(F32)
    for i in range(1, parts_ref.shape[0]):
        total = total + parts_ref[i].astype(F32)
    scale = 1.0 + damping_ref[...]
    for a in range(4):
        rows = slice(8 * a, 8 * a + 8)
        at = (a % 2) * 64 + (a // 2) * 32
        force = jnp.concatenate([total[r][:, at : at + 32] for r in range(2 * N_SAME)], axis=1)
        out_ref[rows, :] = (base_ref[rows, :] - force) / scale


def final_step(parts, base, damping):
    return pl.pallas_call(
        final_kernel,
        out_shape=jax.ShapeDtypeStruct(base.shape, F32),
        compiler_params=pltpu.CompilerParams(vmem_limit_bytes=16 << 20),
        name="final_step",
    )(parts, base, damping)


def exchange(x, axes):
    return lax.all_to_all(x, axes, split_axis=0, concat_axis=0, tiled=True)


def spread(x, axes, n):
    return exchange(jnp.broadcast_to(x[None], (n, *x.shape)), axes)


def swap(x):
    return lax.ppermute(x, "c", [(0, 1), (1, 0)])


def shift(x, by):
    return lax.ppermute(x, "y", [(i, (i + by) % N_Y) for i in range(N_Y)])


def after(x):
    return lax.optimization_barrier(x)


def shards(
    amplitudes, previous, coupling, stiffness, airy_scale, damping, strike_mode, strike_offset
):
    n_k, rows, width = coupling.shape
    y = lax.axis_index("y").astype(jnp.int32)
    core = lax.axis_index("c").astype(jnp.int32)
    same = lax.axis_index(SAME)
    row = lax.axis_index(ROW).astype(jnp.int32).reshape(1)
    half = y % PARTS
    place = jnp.stack([half, core])

    piece = lax.dynamic_slice_in_dim(amplitudes, half * FEW, FEW, 0).astype(BF)
    b0 = spread(piece, SAME, N_SAME).reshape(WIDE, width)
    b1 = [shift(b0[: WIDE // 2], -1), shift(b0[WIDE // 2 :], 1)]
    o0 = swap(b0)
    (i0, j0), (p0, q0) = inner_products(row, coupling, [[b0], [o0]], [F32, BF], 16, True)

    per = n_k // N_SAME
    n_half = PARTS * WIDE
    scale = lax.dynamic_slice_in_dim(airy_scale, same * per, per, 0)
    b1, p0, q0, scale = after((b1, p0, q0, scale))
    o1 = [swap(b) for b in b1]
    (i1,), (p1,) = inner_products(row, coupling, [b1], [F32], 64)

    o1, p1 = after((o1, p1))
    (j1,), (q1,) = inner_products(row, coupling, [o1], [BF], 64)

    part = combine([p0, p1], [swap(q0), swap(q1)])
    shares = exchange(part.reshape(N_SAME, per, n_half), SAME)
    summed = jnp.sum(shares.astype(F32), axis=0) / scale[:, None]
    airy_own = spread(summed.astype(BF), SAME, N_SAME).reshape(n_k, n_half)
    airy_other = swap(airy_own)

    force_own = forces(place, airy_own, [i0, i1])
    messages = forces(place, airy_other, [j0, j1], force_own)
    messages, late = after((messages, (amplitudes, previous, damping, stiffness, strike_mode, strike_offset)))
    amplitudes, previous, damping, stiffness, strike_mode, strike_offset = late
    arrived = exchange(messages.reshape(2 * N_SAME, 8, 128), ROW)
    airy = airy_output(place, airy_own, airy_other).reshape(2 * N_SAME * rows, n_k)

    offset = strike_offset.astype(F32)
    pulse = jnp.where(
        strike_offset <= STRIKE_LEN, 2.0 * (1.0 - jnp.cos(jnp.pi * offset / STRIKE_LEN)), 0.0
    )
    modes = jnp.arange(width, dtype=jnp.int32)
    excite = jnp.where(modes[None, :] == strike_mode[:, None], pulse[:, None], 0.0)
    base = 2.0 * amplitudes - (1.0 - damping) * previous - stiffness * amplitudes + excite

    arrived, airy, base = after((arrived, airy, base))
    parts = spread(arrived, INPLANE, N_IN)
    result = final_step(parts, base, damping[None, :])
    return (result, airy)


def solution(mesh):
    fine = Mesh(mesh.devices.reshape(SIZES), AXES)
    return jax.shard_map(
        shards,
        mesh=fine,
        in_specs=(
            P(ROW, None),
            P(ROW, None),
            P(INPLANE, ROW, None),
            P(),
            P(INPLANE),
            P(),
            P(ROW),
            P(ROW),
        ),
        out_specs=(P(ROW, None), P(None, INPLANE)),
        check_vma=False,
    )
```

```python
import functools

import jax
import jax.numpy as jnp
from jax import lax
from jax.experimental import pallas as pl
from jax.experimental.pallas import tpu as pltpu
from jax.sharding import Mesh, PartitionSpec as P

STRIKE_LEN = 64
AXES = ("xh", "y", "xl", "z", "c")
SIZES = (2, 4, 2, 8, 2)
INPLANE = ("xh", "y")
ROW = ("xl", "z", "c")
SAME = ("xl", "z")
N_IN = 8
N_Y = 4
N_SAME = 16
PARTS = 2
FEW = 16
WIDE = 256
BF = jnp.bfloat16
F32 = jnp.float32


VMEM = pl.BlockSpec(memory_space=pltpu.VMEM)


def in_vmem(x):
    return pltpu.with_memory_space_constraint(x, pltpu.VMEM)


def inner_kernel(counts, slabs, stream, row_ref, tensor_ref, *refs):
    n_in, blocks = sum(counts), len(counts)
    case_refs = refs[:n_in]
    inner_refs = refs[n_in : n_in + blocks]
    part_refs = refs[n_in + blocks : n_in + 2 * blocks]
    turned = refs[-1]
    _, rows, width = tensor_ref.shape
    step = pl.program_id(0)

    @pl.when(step == 0)
    def _():
        at = 0
        for b, count in enumerate(counts):
            pieces = [case_refs[at + i][...] for i in range(count)]
            whole = pieces[0] if count == 1 else jnp.concatenate(pieces, axis=0)
            turned[:, b * WIDE : (b + 1) * WIDE] = whole.T
            at += count

    start = pl.multiple_of(row_ref[0] * rows, rows)
    columns = turned[pl.ds(start, rows), :].astype(F32)
    tensor = tensor_ref[...] if stream else tensor_ref[pl.ds(step * slabs, slabs)]
    inner = jnp.dot(
        tensor.reshape(slabs * rows, width), turned[...], preferred_element_type=F32
    ).reshape(slabs, rows, blocks * WIDE)
    for b in range(blocks):
        span = slice(b * WIDE, (b + 1) * WIDE)
        piece = inner[:, :, span]
        inner_refs[b][...] = piece.astype(BF)
        part = jnp.sum(piece * columns[None, :, span], axis=1)
        at = pl.ds(pl.multiple_of(step * slabs, slabs), slabs)
        part_refs[b][at, :] = part.astype(part_refs[b].dtype)


def inner_products(row, coupling, groups, part_types, slabs=32, stream=False):
    n_k, rows, width = coupling.shape
    counts = tuple(len(g) for g in groups)
    cases = [c for g in groups for c in g]
    blocks = len(groups)
    placed = pltpu.with_memory_space_constraint(coupling, pltpu.HBM if stream else pltpu.VMEM)
    out = pl.pallas_call(
        functools.partial(inner_kernel, counts, slabs, stream),
        grid_spec=pltpu.PrefetchScalarGridSpec(
            num_scalar_prefetch=1,
            grid=(n_k // slabs,),
            in_specs=[pl.BlockSpec((slabs, rows, width), lambda k, r: (k, 0, 0)) if stream else VMEM]
            + [VMEM] * len(cases),
            out_specs=[pl.BlockSpec((slabs, rows, WIDE), lambda k, r: (k, 0, 0))] * blocks
            + [VMEM] * blocks,
            scratch_shapes=[pltpu.VMEM((width, blocks * WIDE), BF)],
        ),
        out_shape=[jax.ShapeDtypeStruct((n_k, rows, WIDE), BF)] * blocks
        + [jax.ShapeDtypeStruct((n_k, WIDE), t) for t in part_types],
        cost_estimate=pl.CostEstimate(
            flops=2 * n_k * rows * width * blocks * WIDE, bytes_accessed=10 << 20, transcendentals=0
        ),
        compiler_params=pltpu.CompilerParams(vmem_limit_bytes=20 << 20),
        name="inner_products",
    )(row, placed, *[in_vmem(c) for c in cases])
    return out[:blocks], out[blocks:]


def combine_kernel(*refs):
    *sources, out_ref = refs
    half = len(sources) // 2
    for b in range(half):
        total = sources[b][...] + sources[half + b][...].astype(F32)
        out_ref[:, b * WIDE : (b + 1) * WIDE] = total.astype(BF)


def combine(mine, received):
    n_k = mine[0].shape[0]
    return pl.pallas_call(
        combine_kernel,
        out_shape=jax.ShapeDtypeStruct((n_k, WIDE * len(mine)), BF),
        compiler_params=pltpu.CompilerParams(vmem_limit_bytes=4 << 20),
        name="combine",
    )(*mine, *received)


def force_kernel(pair, place_ref, airy_ref, *refs):
    if pair:
        *inner_refs, mine_ref, out_ref, total = refs
    else:
        *inner_refs, out_ref, total = refs
    n_k, rows, _ = inner_refs[0].shape
    half, core = place_ref[0], place_ref[1]

    for d, inner_ref in enumerate(inner_refs):
        acc = jnp.zeros((rows, WIDE), F32)
        for k in range(n_k):
            weight = airy_ref[k : k + 1, d * WIDE : (d + 1) * WIDE].astype(F32)
            acc = acc + weight * inner_ref[k].astype(F32)
        at = pl.ds(pl.multiple_of(((half + d) % PARTS) * rows, rows), rows)
        total[at, :] = acc

    turned = total[...].T.reshape(N_SAME, FEW, PARTS * rows)
    turned = jnp.concatenate([turned[:, :8], turned[:, 8:]], axis=2).astype(BF)
    if pair:
        out_ref[:, core] = mine_ref[...]
        out_ref[:, 1 - core] = turned
    else:
        out_ref[...] = turned


def forces(place, airy, inners, mine=None):
    n_k, rows, _ = inners[0].shape
    pair = mine is not None
    shape = (N_SAME, 2, 8, 128) if pair else (N_SAME, 8, 128)
    operands = [airy, *inners] + ([mine] if pair else [])
    return pl.pallas_call(
        functools.partial(force_kernel, pair),
        in_specs=[pl.BlockSpec(memory_space=pltpu.SMEM)] + [VMEM] * len(operands),
        out_specs=VMEM,
        out_shape=jax.ShapeDtypeStruct(shape, BF),
        scratch_shapes=[pltpu.VMEM((PARTS * rows, WIDE), F32)],
        cost_estimate=pl.CostEstimate(
            flops=2 * n_k * rows * airy.shape[1], bytes_accessed=4 << 20, transcendentals=0
        ),
        compiler_params=pltpu.CompilerParams(vmem_limit_bytes=8 << 20),
        name="forces",
    )(place, *[in_vmem(x) for x in operands])


def airy_kernel(place_ref, mine_ref, theirs_ref, out_ref):
    half, core = place_ref[0], place_ref[1]
    for source, at in ((mine_ref, core), (theirs_ref, 1 - core)):
        for d in range(PARTS):
            piece = source[:, d * WIDE : (d + 1) * WIDE].astype(F32).T
            out_ref[:, at, (half + d) % PARTS] = piece.reshape(N_SAME, FEW, piece.shape[1])


def airy_output(place, mine, theirs):
    full = pl.BlockSpec(mine.shape, lambda i, s: (0, 0))
    shape = (N_SAME, 2, PARTS, FEW, mine.shape[0])
    return pl.pallas_call(
        airy_kernel,
        grid_spec=pltpu.PrefetchScalarGridSpec(
            num_scalar_prefetch=1,
            grid=(1,),
            in_specs=[full, full],
            out_specs=pl.BlockSpec(shape, lambda i, s: (0,) * 5),
        ),
        out_shape=jax.ShapeDtypeStruct(shape, F32),
        cost_estimate=pl.CostEstimate(flops=1 << 20, bytes_accessed=1 << 20, transcendentals=0),
        compiler_params=pltpu.CompilerParams(vmem_limit_bytes=8 << 20),
        name="airy_output",
    )(place, mine, theirs)


def final_kernel(parts_ref, base_ref, damping_ref, out_ref):
    total = parts_ref[0].astype(F32)
    for i in range(1, parts_ref.shape[0]):
        total = total + parts_ref[i].astype(F32)
    scale = 1.0 + damping_ref[...]
    for a in range(4):
        rows = slice(8 * a, 8 * a + 8)
        at = (a % 2) * 64 + (a // 2) * 32
        force = jnp.concatenate([total[r][:, at : at + 32] for r in range(2 * N_SAME)], axis=1)
        out_ref[rows, :] = (base_ref[rows, :] - force) / scale


def final_step(parts, base, damping):
    return pl.pallas_call(
        final_kernel,
        out_shape=jax.ShapeDtypeStruct(base.shape, F32),
        compiler_params=pltpu.CompilerParams(vmem_limit_bytes=16 << 20),
        name="final_step",
    )(parts, base, damping)


def exchange(x, axes):
    return lax.all_to_all(x, axes, split_axis=0, concat_axis=0, tiled=True)


def spread(x, axes, n):
    return exchange(jnp.broadcast_to(x[None], (n, *x.shape)), axes)


def swap(x):
    return lax.ppermute(x, "c", [(0, 1), (1, 0)])


def shift(x, by):
    return lax.ppermute(x, "y", [(i, (i + by) % N_Y) for i in range(N_Y)])


def after(x):
    return lax.optimization_barrier(x)


def shards(
    amplitudes, previous, coupling, stiffness, airy_scale, damping, strike_mode, strike_offset
):
    n_k, rows, width = coupling.shape
    y = lax.axis_index("y").astype(jnp.int32)
    core = lax.axis_index("c").astype(jnp.int32)
    same = lax.axis_index(SAME)
    row = lax.axis_index(ROW).astype(jnp.int32).reshape(1)
    half = y % PARTS
    place = jnp.stack([half, core])

    per = n_k // N_SAME
    n_half = PARTS * WIDE
    piece = lax.dynamic_slice_in_dim(amplitudes, half * FEW, FEW, 0).astype(BF)
    scale = lax.dynamic_slice_in_dim(airy_scale, same * per, per, 0)
    piece, scale, row, place = after((piece, scale, row, place))
    b0 = spread(piece, SAME, N_SAME).reshape(WIDE, width)
    b1 = [shift(b0[: WIDE // 2], -1), shift(b0[WIDE // 2 :], 1)]
    o0 = swap(b0)
    (i0, j0), (p0, q0) = inner_products(row, coupling, [[b0], [o0]], [F32, BF])

    b1, p0, q0 = after((b1, p0, q0))
    o1 = [swap(b) for b in b1]
    (i1,), (p1,) = inner_products(row, coupling, [b1], [F32], 64)

    o1, p1 = after((o1, p1))
    (j1,), (q1,) = inner_products(row, coupling, [o1], [BF], 64)

    part = combine([p0, p1], [swap(q0), swap(q1)])
    shares = exchange(part.reshape(N_SAME, per, n_half), SAME)
    summed = jnp.sum(shares.astype(F32), axis=0) / scale[:, None]
    airy_own = spread(summed.astype(BF), SAME, N_SAME).reshape(n_k, n_half)
    airy_other = swap(airy_own)

    force_own = forces(place, airy_own, [i0, i1])
    messages = forces(place, airy_other, [j0, j1], force_own)
    messages, late = after((messages, (amplitudes, previous, damping, stiffness, strike_mode, strike_offset)))
    amplitudes, previous, damping, stiffness, strike_mode, strike_offset = late
    arrived = exchange(messages.reshape(2 * N_SAME, 8, 128), ROW)
    airy = airy_output(place, airy_own, airy_other).reshape(2 * N_SAME * rows, n_k)

    offset = strike_offset.astype(F32)
    pulse = jnp.where(
        strike_offset <= STRIKE_LEN, 2.0 * (1.0 - jnp.cos(jnp.pi * offset / STRIKE_LEN)), 0.0
    )
    modes = jnp.arange(width, dtype=jnp.int32)
    excite = jnp.where(modes[None, :] == strike_mode[:, None], pulse[:, None], 0.0)
    base = 2.0 * amplitudes - (1.0 - damping) * previous - stiffness * amplitudes + excite

    arrived, airy, base = after((arrived, airy, base))
    parts = spread(arrived, INPLANE, N_IN)
    result = final_step(parts, base, damping[None, :])
    return (result, airy)


def solution(mesh):
    fine = Mesh(mesh.devices.reshape(SIZES), AXES)
    return jax.shard_map(
        shards,
        mesh=fine,
        in_specs=(
            P(ROW, None),
            P(ROW, None),
            P(INPLANE, ROW, None),
            P(),
            P(INPLANE),
            P(),
            P(ROW),
            P(ROW),
        ),
        out_specs=(P(ROW, None), P(None, INPLANE)),
        check_vma=False,
    )
```

```python
import functools

import jax
import jax.numpy as jnp
from jax import lax
from jax.experimental import pallas as pl
from jax.experimental.pallas import tpu as pltpu
from jax.sharding import Mesh, PartitionSpec as P

STRIKE_LEN = 64
AXES = ("xh", "y", "xl", "z", "c")
SIZES = (2, 4, 2, 8, 2)
INPLANE = ("xh", "y")
ROW = ("xl", "z", "c")
SAME = ("xl", "z")
N_IN = 8
N_Y = 4
N_SAME = 16
PARTS = 2
FEW = 16
WIDE = 256
BF = jnp.bfloat16
F32 = jnp.float32


VMEM = pl.BlockSpec(memory_space=pltpu.VMEM)


def in_vmem(x):
    return pltpu.with_memory_space_constraint(x, pltpu.VMEM)


def inner_kernel(counts, slabs, stream, row_ref, tensor_ref, *refs):
    n_in, blocks = sum(counts), len(counts)
    case_refs = refs[:n_in]
    inner_refs = refs[n_in : n_in + blocks]
    part_refs = refs[n_in + blocks : n_in + 2 * blocks]
    turned = refs[-1]
    _, rows, width = tensor_ref.shape
    step = pl.program_id(0)

    @pl.when(step == 0)
    def _():
        at = 0
        for b, count in enumerate(counts):
            pieces = [case_refs[at + i][...] for i in range(count)]
            whole = pieces[0] if count == 1 else jnp.concatenate(pieces, axis=0)
            turned[:, b * WIDE : (b + 1) * WIDE] = whole.T
            at += count

    start = pl.multiple_of(row_ref[0] * rows, rows)
    columns = turned[pl.ds(start, rows), :].astype(F32)
    tensor = tensor_ref[...] if stream else tensor_ref[pl.ds(step * slabs, slabs)]
    inner = jnp.dot(
        tensor.reshape(slabs * rows, width), turned[...], preferred_element_type=F32
    ).reshape(slabs, rows, blocks * WIDE)
    for b in range(blocks):
        span = slice(b * WIDE, (b + 1) * WIDE)
        piece = inner[:, :, span]
        inner_refs[b][...] = piece.astype(BF)
        part = jnp.sum(piece * columns[None, :, span], axis=1)
        at = pl.ds(pl.multiple_of(step * slabs, slabs), slabs)
        part_refs[b][at, :] = part.astype(part_refs[b].dtype)


def inner_products(row, coupling, groups, part_types, slabs=32, stream=False):
    n_k, rows, width = coupling.shape
    counts = tuple(len(g) for g in groups)
    cases = [c for g in groups for c in g]
    blocks = len(groups)
    placed = pltpu.with_memory_space_constraint(coupling, pltpu.HBM if stream else pltpu.VMEM)
    out = pl.pallas_call(
        functools.partial(inner_kernel, counts, slabs, stream),
        grid_spec=pltpu.PrefetchScalarGridSpec(
            num_scalar_prefetch=1,
            grid=(n_k // slabs,),
            in_specs=[pl.BlockSpec((slabs, rows, width), lambda k, r: (k, 0, 0)) if stream else VMEM]
            + [VMEM] * len(cases),
            out_specs=[pl.BlockSpec((slabs, rows, WIDE), lambda k, r: (k, 0, 0))] * blocks
            + [VMEM] * blocks,
            scratch_shapes=[pltpu.VMEM((width, blocks * WIDE), BF)],
        ),
        out_shape=[jax.ShapeDtypeStruct((n_k, rows, WIDE), BF)] * blocks
        + [jax.ShapeDtypeStruct((n_k, WIDE), t) for t in part_types],
        cost_estimate=pl.CostEstimate(
            flops=2 * n_k * rows * width * blocks * WIDE, bytes_accessed=10 << 20, transcendentals=0
        ),
        compiler_params=pltpu.CompilerParams(vmem_limit_bytes=20 << 20),
        name="inner_products",
    )(row, placed, *[in_vmem(c) for c in cases])
    return out[:blocks], out[blocks:]


def spread_kernel(place_ref, piece_ref, out_ref):
    piece = piece_ref[...].astype(BF)
    for g in range(N_SAME):
        out_ref[g] = piece


def spread_piece(place, amplitudes):
    width = amplitudes.shape[1]
    return pl.pallas_call(
        spread_kernel,
        grid_spec=pltpu.PrefetchScalarGridSpec(
            num_scalar_prefetch=1,
            grid=(1,),
            in_specs=[pl.BlockSpec((FEW, width), lambda i, s: (s[0], 0))],
            out_specs=VMEM,
        ),
        out_shape=jax.ShapeDtypeStruct((N_SAME, FEW, width), BF),
        cost_estimate=pl.CostEstimate(flops=1 << 34, bytes_accessed=1 << 20, transcendentals=0),
        compiler_params=pltpu.CompilerParams(vmem_limit_bytes=4 << 20),
        name="spread_piece",
    )(place, pltpu.with_memory_space_constraint(amplitudes, pltpu.HBM))


def combine_kernel(scale_ref, *refs):
    *sources, out_ref = refs
    half = len(sources) // 2
    n_k = out_ref.shape[0]
    scale = jnp.broadcast_to(scale_ref[...], (n_k, n_k)).T
    scale = jnp.concatenate([scale] * (WIDE // n_k), axis=1)
    for b in range(half):
        total = sources[b][...] + sources[half + b][...].astype(F32)
        out_ref[:, b * WIDE : (b + 1) * WIDE] = (total / scale).astype(BF)


def combine(airy_scale, mine, received):
    n_k = mine[0].shape[0]
    return pl.pallas_call(
        combine_kernel,
        out_shape=jax.ShapeDtypeStruct((n_k, WIDE * len(mine)), BF),
        compiler_params=pltpu.CompilerParams(vmem_limit_bytes=4 << 20),
        name="combine",
    )(airy_scale[None, :], *mine, *received)


def total_kernel(shares_ref, out_ref):
    total = shares_ref[0].astype(F32)
    for g in range(1, N_SAME):
        total = total + shares_ref[g].astype(F32)
    total = total.astype(BF)
    for g in range(N_SAME):
        out_ref[g] = total


def total_everywhere(shares):
    return pl.pallas_call(
        total_kernel,
        out_shape=jax.ShapeDtypeStruct(shares.shape, BF),
        compiler_params=pltpu.CompilerParams(vmem_limit_bytes=4 << 20),
        name="total_everywhere",
    )(shares)


def force_kernel(pair, place_ref, airy_ref, *refs):
    if pair:
        *inner_refs, mine_ref, out_ref, total = refs
    else:
        *inner_refs, out_ref, total = refs
    n_k, rows, _ = inner_refs[0].shape
    half, core = place_ref[0], place_ref[1]

    for d, inner_ref in enumerate(inner_refs):
        acc = jnp.zeros((rows, WIDE), F32)
        for k in range(n_k):
            weight = airy_ref[k : k + 1, d * WIDE : (d + 1) * WIDE].astype(F32)
            acc = acc + weight * inner_ref[k].astype(F32)
        at = pl.ds(pl.multiple_of(((half + d) % PARTS) * rows, rows), rows)
        total[at, :] = acc

    turned = total[...].T.reshape(N_SAME, FEW, PARTS * rows)
    turned = jnp.concatenate([turned[:, :8], turned[:, 8:]], axis=2).astype(BF)
    if pair:
        out_ref[:, core] = mine_ref[...]
        out_ref[:, 1 - core] = turned
    else:
        out_ref[...] = turned


def forces(place, airy, inners, mine=None):
    n_k, rows, _ = inners[0].shape
    pair = mine is not None
    shape = (N_SAME, 2, 8, 128) if pair else (N_SAME, 8, 128)
    operands = [airy, *inners] + ([mine] if pair else [])
    return pl.pallas_call(
        functools.partial(force_kernel, pair),
        in_specs=[pl.BlockSpec(memory_space=pltpu.SMEM)] + [VMEM] * len(operands),
        out_specs=VMEM,
        out_shape=jax.ShapeDtypeStruct(shape, BF),
        scratch_shapes=[pltpu.VMEM((PARTS * rows, WIDE), F32)],
        cost_estimate=pl.CostEstimate(
            flops=2 * n_k * rows * airy.shape[1], bytes_accessed=4 << 20, transcendentals=0
        ),
        compiler_params=pltpu.CompilerParams(vmem_limit_bytes=8 << 20),
        name="forces",
    )(place, *[in_vmem(x) for x in operands])


def airy_kernel(place_ref, mine_ref, theirs_ref, out_ref):
    half, core = place_ref[0], place_ref[1]
    for source, at in ((mine_ref, core), (theirs_ref, 1 - core)):
        for d in range(PARTS):
            piece = source[:, d * WIDE : (d + 1) * WIDE].astype(F32).T
            out_ref[:, at, (half + d) % PARTS] = piece.reshape(N_SAME, FEW, piece.shape[1])


def airy_output(place, mine, theirs):
    full = pl.BlockSpec(mine.shape, lambda i, s: (0, 0))
    shape = (N_SAME, 2, PARTS, FEW, mine.shape[0])
    return pl.pallas_call(
        airy_kernel,
        grid_spec=pltpu.PrefetchScalarGridSpec(
            num_scalar_prefetch=1,
            grid=(1,),
            in_specs=[full, full],
            out_specs=pl.BlockSpec(shape, lambda i, s: (0,) * 5),
        ),
        out_shape=jax.ShapeDtypeStruct(shape, F32),
        cost_estimate=pl.CostEstimate(flops=1 << 20, bytes_accessed=1 << 20, transcendentals=0),
        compiler_params=pltpu.CompilerParams(vmem_limit_bytes=8 << 20),
        name="airy_output",
    )(place, mine, theirs)


def final_kernel(parts_ref, base_ref, damping_ref, out_ref):
    total = parts_ref[0].astype(F32)
    for i in range(1, parts_ref.shape[0]):
        total = total + parts_ref[i].astype(F32)
    scale = 1.0 + damping_ref[...]
    for a in range(4):
        rows = slice(8 * a, 8 * a + 8)
        at = (a % 2) * 64 + (a // 2) * 32
        force = jnp.concatenate([total[r][:, at : at + 32] for r in range(2 * N_SAME)], axis=1)
        out_ref[rows, :] = (base_ref[rows, :] - force) / scale


def final_step(parts, base, damping):
    return pl.pallas_call(
        final_kernel,
        out_shape=jax.ShapeDtypeStruct(base.shape, F32),
        compiler_params=pltpu.CompilerParams(vmem_limit_bytes=16 << 20),
        name="final_step",
    )(parts, base, damping)


def exchange(x, axes):
    return lax.all_to_all(x, axes, split_axis=0, concat_axis=0, tiled=True)


def spread(x, axes, n):
    return exchange(jnp.broadcast_to(x[None], (n, *x.shape)), axes)


def swap(x):
    return lax.ppermute(x, "c", [(0, 1), (1, 0)])


def shift(x, by):
    return lax.ppermute(x, "y", [(i, (i + by) % N_Y) for i in range(N_Y)])


def after(x):
    return lax.optimization_barrier(x)


def shards(
    amplitudes, previous, coupling, stiffness, airy_scale, damping, strike_mode, strike_offset
):
    n_k, rows, width = coupling.shape
    y = lax.axis_index("y").astype(jnp.int32)
    core = lax.axis_index("c").astype(jnp.int32)
    row = lax.axis_index(ROW).astype(jnp.int32).reshape(1)
    half = y % PARTS
    place = jnp.stack([half, core])

    per = n_k // N_SAME
    n_half = PARTS * WIDE
    row, place = after((row, place))
    piece, row, place = after((spread_piece(place, amplitudes), row, place))
    b0 = exchange(piece, SAME).reshape(WIDE, width)
    b1 = [shift(b0[: WIDE // 2], -1), shift(b0[WIDE // 2 :], 1)]
    o0 = swap(b0)
    (i0, j0), (p0, q0) = inner_products(row, coupling, [[b0], [o0]], [F32, BF])

    b1, p0, q0 = after((b1, p0, q0))
    o1 = [swap(b) for b in b1]
    (i1,), (p1,) = inner_products(row, coupling, [b1], [F32], 64)

    o1, p1 = after((o1, p1))
    (j1,), (q1,) = inner_products(row, coupling, [o1], [BF], 64)

    part = combine(airy_scale, [p0, p1], [swap(q0), swap(q1)])
    shares = exchange(part.reshape(N_SAME, per, n_half), SAME)
    airy_own = exchange(total_everywhere(shares), SAME).reshape(n_k, n_half)
    airy_other = swap(airy_own)

    force_own = forces(place, airy_own, [i0, i1])
    messages = forces(place, airy_other, [j0, j1], force_own)
    messages, late = after((messages, (amplitudes, previous, damping, stiffness, strike_mode, strike_offset)))
    amplitudes, previous, damping, stiffness, strike_mode, strike_offset = late
    arrived = exchange(messages.reshape(2 * N_SAME, 8, 128), ROW)
    airy = airy_output(place, airy_own, airy_other).reshape(2 * N_SAME * rows, n_k)

    offset = strike_offset.astype(F32)
    pulse = jnp.where(
        strike_offset <= STRIKE_LEN, 2.0 * (1.0 - jnp.cos(jnp.pi * offset / STRIKE_LEN)), 0.0
    )
    modes = jnp.arange(width, dtype=jnp.int32)
    excite = jnp.where(modes[None, :] == strike_mode[:, None], pulse[:, None], 0.0)
    base = 2.0 * amplitudes - (1.0 - damping) * previous - stiffness * amplitudes + excite

    arrived, airy, base = after((arrived, airy, base))
    parts = spread(arrived, INPLANE, N_IN)
    result = final_step(parts, base, damping[None, :])
    return (result, airy)


def solution(mesh):
    fine = Mesh(mesh.devices.reshape(SIZES), AXES)
    return jax.shard_map(
        shards,
        mesh=fine,
        in_specs=(
            P(ROW, None),
            P(ROW, None),
            P(INPLANE, ROW, None),
            P(),
            P(INPLANE),
            P(),
            P(ROW),
            P(ROW),
        ),
        out_specs=(P(ROW, None), P(None, INPLANE)),
        check_vma=False,
    )
```

```python
import functools

import jax
import jax.numpy as jnp
from jax import lax
from jax.experimental import pallas as pl
from jax.experimental.pallas import tpu as pltpu
from jax.sharding import Mesh, PartitionSpec as P

STRIKE_LEN = 64
AXES = ("xh", "y", "xl", "z", "c")
SIZES = (2, 4, 2, 8, 2)
INPLANE = ("xh", "y")
ROW = ("xl", "z", "c")
SAME = ("xl", "z")
N_IN = 8
N_Y = 4
N_SAME = 16
PARTS = 2
FEW = 16
WIDE = 256
BF = jnp.bfloat16
F32 = jnp.float32


VMEM = pl.BlockSpec(memory_space=pltpu.VMEM)


def in_vmem(x):
    return pltpu.with_memory_space_constraint(x, pltpu.VMEM)


def inner_kernel(counts, slabs, stream, row_ref, tensor_ref, *refs):
    n_in, blocks = sum(counts), len(counts)
    case_refs = refs[:n_in]
    inner_refs = refs[n_in : n_in + blocks]
    part_refs = refs[n_in + blocks : n_in + 2 * blocks]
    turned = refs[-1]
    _, rows, width = tensor_ref.shape
    step = pl.program_id(0)

    @pl.when(step == 0)
    def _():
        at = 0
        for b, count in enumerate(counts):
            pieces = [case_refs[at + i][...] for i in range(count)]
            whole = pieces[0] if count == 1 else jnp.concatenate(pieces, axis=0)
            turned[:, b * WIDE : (b + 1) * WIDE] = whole.T
            at += count

    start = pl.multiple_of(row_ref[0] * rows, rows)
    columns = turned[pl.ds(start, rows), :].astype(F32)
    tensor = tensor_ref[...] if stream else tensor_ref[pl.ds(step * slabs, slabs)]
    inner = jnp.dot(
        tensor.reshape(slabs * rows, width), turned[...], preferred_element_type=F32
    ).reshape(slabs, rows, blocks * WIDE)
    for b in range(blocks):
        span = slice(b * WIDE, (b + 1) * WIDE)
        piece = inner[:, :, span]
        inner_refs[b][...] = piece.astype(BF)
        part = jnp.sum(piece * columns[None, :, span], axis=1)
        at = pl.ds(pl.multiple_of(step * slabs, slabs), slabs)
        part_refs[b][at, :] = part.astype(part_refs[b].dtype)


def inner_products(row, coupling, groups, part_types, slabs=32, stream=False):
    n_k, rows, width = coupling.shape
    counts = tuple(len(g) for g in groups)
    cases = [c for g in groups for c in g]
    blocks = len(groups)
    placed = pltpu.with_memory_space_constraint(coupling, pltpu.HBM if stream else pltpu.VMEM)
    out = pl.pallas_call(
        functools.partial(inner_kernel, counts, slabs, stream),
        grid_spec=pltpu.PrefetchScalarGridSpec(
            num_scalar_prefetch=1,
            grid=(n_k // slabs,),
            in_specs=[pl.BlockSpec((slabs, rows, width), lambda k, r: (k, 0, 0)) if stream else VMEM]
            + [VMEM] * len(cases),
            out_specs=[pl.BlockSpec((slabs, rows, WIDE), lambda k, r: (k, 0, 0))] * blocks
            + [VMEM] * blocks,
            scratch_shapes=[pltpu.VMEM((width, blocks * WIDE), BF)],
        ),
        out_shape=[jax.ShapeDtypeStruct((n_k, rows, WIDE), BF)] * blocks
        + [jax.ShapeDtypeStruct((n_k, WIDE), t) for t in part_types],
        cost_estimate=pl.CostEstimate(
            flops=2 * n_k * rows * width * blocks * WIDE, bytes_accessed=10 << 20, transcendentals=0
        ),
        compiler_params=pltpu.CompilerParams(vmem_limit_bytes=20 << 20),
        name="inner_products",
    )(row, placed, *[in_vmem(c) for c in cases])
    return out[:blocks], out[blocks:]


def spread_kernel(place_ref, piece_ref, out_ref):
    piece = piece_ref[...].astype(BF)
    for g in range(N_SAME):
        out_ref[g] = piece


def spread_piece(place, amplitudes):
    width = amplitudes.shape[1]
    return pl.pallas_call(
        spread_kernel,
        grid_spec=pltpu.PrefetchScalarGridSpec(
            num_scalar_prefetch=1,
            grid=(1,),
            in_specs=[pl.BlockSpec((FEW, width), lambda i, s: (s[0], 0))],
            out_specs=VMEM,
        ),
        out_shape=jax.ShapeDtypeStruct((N_SAME, FEW, width), BF),
        cost_estimate=pl.CostEstimate(flops=1 << 34, bytes_accessed=1 << 20, transcendentals=0),
        compiler_params=pltpu.CompilerParams(vmem_limit_bytes=4 << 20),
        name="spread_piece",
    )(place, pltpu.with_memory_space_constraint(amplitudes, pltpu.HBM))


def combine_kernel(scale_ref, *refs):
    *sources, out_ref = refs
    half = len(sources) // 2
    n_k = out_ref.shape[0]
    scale = jnp.broadcast_to(scale_ref[...], (n_k, n_k)).T
    scale = jnp.concatenate([scale] * (WIDE // n_k), axis=1)
    for b in range(half):
        total = sources[b][...] + sources[half + b][...].astype(F32)
        out_ref[:, b * WIDE : (b + 1) * WIDE] = (total / scale).astype(BF)


def combine(airy_scale, mine, received):
    n_k = mine[0].shape[0]
    return pl.pallas_call(
        combine_kernel,
        out_shape=jax.ShapeDtypeStruct((n_k, WIDE * len(mine)), BF),
        compiler_params=pltpu.CompilerParams(vmem_limit_bytes=4 << 20),
        name="combine",
    )(airy_scale[None, :], *mine, *received)


def total_kernel(shares_ref, out_ref):
    total = shares_ref[0].astype(F32)
    for g in range(1, N_SAME):
        total = total + shares_ref[g].astype(F32)
    total = total.astype(BF)
    for g in range(N_SAME):
        out_ref[g] = total


def total_everywhere(shares):
    return pl.pallas_call(
        total_kernel,
        out_shape=jax.ShapeDtypeStruct(shares.shape, BF),
        compiler_params=pltpu.CompilerParams(vmem_limit_bytes=4 << 20),
        name="total_everywhere",
    )(shares)


def force_kernel(pair, place_ref, airy_ref, *refs):
    if pair:
        *inner_refs, mine_ref, out_ref, total, weights = refs
    else:
        *inner_refs, out_ref, total, weights = refs
    n_k, rows, _ = inner_refs[0].shape
    half, core = place_ref[0], place_ref[1]
    weights[...] = airy_ref[...].astype(F32)

    for d, inner_ref in enumerate(inner_refs):
        acc = jnp.zeros((rows, WIDE), F32)
        for k in range(n_k):
            weight = weights[k : k + 1, d * WIDE : (d + 1) * WIDE]
            acc = acc + weight * inner_ref[k].astype(F32)
        at = pl.ds(pl.multiple_of(((half + d) % PARTS) * rows, rows), rows)
        total[at, :] = acc

    turned = total[...].T.reshape(N_SAME, FEW, PARTS * rows)
    turned = jnp.concatenate([turned[:, :8], turned[:, 8:]], axis=2).astype(BF)
    if pair:
        out_ref[:, core] = mine_ref[...]
        out_ref[:, 1 - core] = turned
    else:
        out_ref[...] = turned


def forces(place, airy, inners, mine=None):
    n_k, rows, _ = inners[0].shape
    pair = mine is not None
    shape = (N_SAME, 2, 8, 128) if pair else (N_SAME, 8, 128)
    operands = [airy, *inners] + ([mine] if pair else [])
    return pl.pallas_call(
        functools.partial(force_kernel, pair),
        in_specs=[pl.BlockSpec(memory_space=pltpu.SMEM)] + [VMEM] * len(operands),
        out_specs=VMEM,
        out_shape=jax.ShapeDtypeStruct(shape, BF),
        scratch_shapes=[pltpu.VMEM((PARTS * rows, WIDE), F32), pltpu.VMEM(airy.shape, F32)],
        cost_estimate=pl.CostEstimate(
            flops=2 * n_k * rows * airy.shape[1], bytes_accessed=4 << 20, transcendentals=0
        ),
        compiler_params=pltpu.CompilerParams(vmem_limit_bytes=8 << 20),
        name="forces",
    )(place, *[in_vmem(x) for x in operands])


def airy_kernel(place_ref, mine_ref, theirs_ref, out_ref):
    half, core = place_ref[0], place_ref[1]
    for source, at in ((mine_ref, core), (theirs_ref, 1 - core)):
        for d in range(PARTS):
            piece = source[:, d * WIDE : (d + 1) * WIDE].astype(F32).T
            out_ref[:, at, (half + d) % PARTS] = piece.reshape(N_SAME, FEW, piece.shape[1])


def airy_output(place, mine, theirs):
    full = pl.BlockSpec(mine.shape, lambda i, s: (0, 0))
    shape = (N_SAME, 2, PARTS, FEW, mine.shape[0])
    return pl.pallas_call(
        airy_kernel,
        grid_spec=pltpu.PrefetchScalarGridSpec(
            num_scalar_prefetch=1,
            grid=(1,),
            in_specs=[full, full],
            out_specs=pl.BlockSpec(shape, lambda i, s: (0,) * 5),
        ),
        out_shape=jax.ShapeDtypeStruct(shape, F32),
        cost_estimate=pl.CostEstimate(flops=1 << 20, bytes_accessed=1 << 20, transcendentals=0),
        compiler_params=pltpu.CompilerParams(vmem_limit_bytes=8 << 20),
        name="airy_output",
    )(place, mine, theirs)


def final_kernel(parts_ref, base_ref, damping_ref, out_ref):
    total = parts_ref[0].astype(F32)
    for i in range(1, parts_ref.shape[0]):
        total = total + parts_ref[i].astype(F32)
    scale = 1.0 + damping_ref[...]
    for a in range(4):
        rows = slice(8 * a, 8 * a + 8)
        at = (a % 2) * 64 + (a // 2) * 32
        force = jnp.concatenate([total[r][:, at : at + 32] for r in range(2 * N_SAME)], axis=1)
        out_ref[rows, :] = (base_ref[rows, :] - force) / scale


def final_step(parts, base, damping):
    return pl.pallas_call(
        final_kernel,
        out_shape=jax.ShapeDtypeStruct(base.shape, F32),
        compiler_params=pltpu.CompilerParams(vmem_limit_bytes=16 << 20),
        name="final_step",
    )(parts, base, damping)


def exchange(x, axes):
    return lax.all_to_all(x, axes, split_axis=0, concat_axis=0, tiled=True)


def spread(x, axes, n):
    return exchange(jnp.broadcast_to(x[None], (n, *x.shape)), axes)


def swap(x):
    return lax.ppermute(x, "c", [(0, 1), (1, 0)])


def shift(x, by):
    return lax.ppermute(x, "y", [(i, (i + by) % N_Y) for i in range(N_Y)])


def after(x):
    return lax.optimization_barrier(x)


def shards(
    amplitudes, previous, coupling, stiffness, airy_scale, damping, strike_mode, strike_offset
):
    n_k, rows, width = coupling.shape
    y = lax.axis_index("y").astype(jnp.int32)
    core = lax.axis_index("c").astype(jnp.int32)
    row = lax.axis_index(ROW).astype(jnp.int32).reshape(1)
    half = y % PARTS
    place = jnp.stack([half, core])

    per = n_k // N_SAME
    n_half = PARTS * WIDE
    row, place = after((row, place))
    piece, row, place = after((spread_piece(place, amplitudes), row, place))
    b0 = exchange(piece, SAME).reshape(WIDE, width)
    b1 = [shift(b0[: WIDE // 2], -1), shift(b0[WIDE // 2 :], 1)]
    (i0,), (p0,) = inner_products(row, coupling, [[b0]], [F32], 64)

    b0, p0 = after((b0, p0))
    o0 = swap(b0)
    (j0,), (q0,) = inner_products(row, coupling, [[o0]], [BF], 64)

    b1, p0, q0 = after((b1, p0, q0))
    o1 = [swap(b) for b in b1]
    (i1,), (p1,) = inner_products(row, coupling, [b1], [F32], 64)

    o1, p1 = after((o1, p1))
    (j1,), (q1,) = inner_products(row, coupling, [o1], [BF], 64)

    part = combine(airy_scale, [p0, p1], [swap(q0), swap(q1)])
    shares = exchange(part.reshape(N_SAME, per, n_half), SAME)
    airy_own = exchange(total_everywhere(shares), SAME).reshape(n_k, n_half)
    airy_other = swap(airy_own)

    force_own = forces(place, airy_own, [i0, i1])
    messages = forces(place, airy_other, [j0, j1], force_own)
    messages, late = after((messages, (amplitudes, previous, damping, stiffness, strike_mode, strike_offset)))
    amplitudes, previous, damping, stiffness, strike_mode, strike_offset = late
    arrived = exchange(messages.reshape(2 * N_SAME, 8, 128), ROW)
    airy = airy_output(place, airy_own, airy_other).reshape(2 * N_SAME * rows, n_k)

    offset = strike_offset.astype(F32)
    pulse = jnp.where(
        strike_offset <= STRIKE_LEN, 2.0 * (1.0 - jnp.cos(jnp.pi * offset / STRIKE_LEN)), 0.0
    )
    modes = jnp.arange(width, dtype=jnp.int32)
    excite = jnp.where(modes[None, :] == strike_mode[:, None], pulse[:, None], 0.0)
    base = 2.0 * amplitudes - (1.0 - damping) * previous - stiffness * amplitudes + excite

    arrived, airy, base = after((arrived, airy, base))
    parts = spread(arrived, INPLANE, N_IN)
    result = final_step(parts, base, damping[None, :])
    return (result, airy)


def solution(mesh):
    fine = Mesh(mesh.devices.reshape(SIZES), AXES)
    return jax.shard_map(
        shards,
        mesh=fine,
        in_specs=(
            P(ROW, None),
            P(ROW, None),
            P(INPLANE, ROW, None),
            P(),
            P(INPLANE),
            P(),
            P(ROW),
            P(ROW),
        ),
        out_specs=(P(ROW, None), P(None, INPLANE)),
        check_vma=False,
    )
```

```python
import functools

import jax
import jax.numpy as jnp
from jax import lax
from jax.experimental import pallas as pl
from jax.experimental.pallas import tpu as pltpu
from jax.sharding import Mesh, PartitionSpec as P

STRIKE_LEN = 64
AXES = ("xh", "y", "xl", "z", "c")
SIZES = (2, 4, 2, 8, 2)
INPLANE = ("xh", "y")
ROW = ("xl", "z", "c")
SAME = ("xl", "z")
N_IN = 8
N_Y = 4
N_SAME = 16
PARTS = 2
FEW = 16
WIDE = 256
BF = jnp.bfloat16
F32 = jnp.float32


VMEM = pl.BlockSpec(memory_space=pltpu.VMEM)


def in_vmem(x):
    return pltpu.with_memory_space_constraint(x, pltpu.VMEM)


def inner_kernel(counts, slabs, stream, row_ref, tensor_ref, *refs):
    n_in, blocks = sum(counts), len(counts)
    case_refs = refs[:n_in]
    inner_refs = refs[n_in : n_in + blocks]
    part_refs = refs[n_in + blocks : n_in + 2 * blocks]
    turned = refs[-1]
    _, rows, width = tensor_ref.shape
    step = pl.program_id(0)

    @pl.when(step == 0)
    def _():
        at = 0
        for b, count in enumerate(counts):
            pieces = [case_refs[at + i][...] for i in range(count)]
            whole = pieces[0] if count == 1 else jnp.concatenate(pieces, axis=0)
            turned[:, b * WIDE : (b + 1) * WIDE] = whole.T
            at += count

    start = pl.multiple_of(row_ref[0] * rows, rows)
    columns = turned[pl.ds(start, rows), :].astype(F32)
    tensor = tensor_ref[...] if stream else tensor_ref[pl.ds(step * slabs, slabs)]
    inner = jnp.dot(
        tensor.reshape(slabs * rows, width), turned[...], preferred_element_type=F32
    ).reshape(slabs, rows, blocks * WIDE)
    for b in range(blocks):
        span = slice(b * WIDE, (b + 1) * WIDE)
        piece = inner[:, :, span]
        inner_refs[b][...] = piece.astype(BF)
        part = jnp.sum(piece * columns[None, :, span], axis=1)
        at = pl.ds(pl.multiple_of(step * slabs, slabs), slabs)
        part_refs[b][at, :] = part.astype(part_refs[b].dtype)


def inner_products(row, coupling, groups, part_types, slabs=32, stream=False):
    n_k, rows, width = coupling.shape
    counts = tuple(len(g) for g in groups)
    cases = [c for g in groups for c in g]
    blocks = len(groups)
    placed = pltpu.with_memory_space_constraint(coupling, pltpu.HBM if stream else pltpu.VMEM)
    out = pl.pallas_call(
        functools.partial(inner_kernel, counts, slabs, stream),
        grid_spec=pltpu.PrefetchScalarGridSpec(
            num_scalar_prefetch=1,
            grid=(n_k // slabs,),
            in_specs=[pl.BlockSpec((slabs, rows, width), lambda k, r: (k, 0, 0)) if stream else VMEM]
            + [VMEM] * len(cases),
            out_specs=[pl.BlockSpec((slabs, rows, WIDE), lambda k, r: (k, 0, 0))] * blocks
            + [VMEM] * blocks,
            scratch_shapes=[pltpu.VMEM((width, blocks * WIDE), BF)],
        ),
        out_shape=[jax.ShapeDtypeStruct((n_k, rows, WIDE), BF)] * blocks
        + [jax.ShapeDtypeStruct((n_k, WIDE), t) for t in part_types],
        cost_estimate=pl.CostEstimate(
            flops=2 * n_k * rows * width * blocks * WIDE, bytes_accessed=10 << 20, transcendentals=0
        ),
        compiler_params=pltpu.CompilerParams(vmem_limit_bytes=20 << 20),
        name="inner_products",
    )(row, placed, *[in_vmem(c) for c in cases])
    return out[:blocks], out[blocks:]


def split_kernel(whole_ref, *out_refs):
    for i, out_ref in enumerate(out_refs):
        out_ref[...] = whole_ref[i * WIDE // 2 : (i + 1) * WIDE // 2, :]


def split(whole):
    half = jax.ShapeDtypeStruct((WIDE // 2, whole.shape[1]), BF)
    return pl.pallas_call(
        split_kernel,
        in_specs=[VMEM],
        out_specs=[VMEM] * 2,
        out_shape=[half] * 2,
        cost_estimate=pl.CostEstimate(flops=1 << 34, bytes_accessed=1 << 20, transcendentals=0),
        compiler_params=pltpu.CompilerParams(vmem_limit_bytes=4 << 20),
        name="split",
    )(whole)


def combine_kernel(scale_ref, *refs):
    *sources, out_ref = refs
    half = len(sources) // 2
    n_k = out_ref.shape[0]
    scale = jnp.broadcast_to(scale_ref[...], (n_k, n_k)).T
    scale = jnp.concatenate([scale] * (WIDE // n_k), axis=1)
    for b in range(half):
        total = sources[b][...] + sources[half + b][...].astype(F32)
        out_ref[:, b * WIDE : (b + 1) * WIDE] = (total / scale).astype(BF)


def combine(airy_scale, mine, received):
    n_k = mine[0].shape[0]
    return pl.pallas_call(
        combine_kernel,
        out_shape=jax.ShapeDtypeStruct((n_k, WIDE * len(mine)), BF),
        compiler_params=pltpu.CompilerParams(vmem_limit_bytes=4 << 20),
        name="combine",
    )(airy_scale[None, :], *mine, *received)


def total_kernel(shares_ref, out_ref):
    total = shares_ref[0].astype(F32)
    for g in range(1, N_SAME):
        total = total + shares_ref[g].astype(F32)
    total = total.astype(BF)
    for g in range(N_SAME):
        out_ref[g] = total


def total_everywhere(shares):
    return pl.pallas_call(
        total_kernel,
        out_shape=jax.ShapeDtypeStruct(shares.shape, BF),
        compiler_params=pltpu.CompilerParams(vmem_limit_bytes=4 << 20),
        name="total_everywhere",
    )(shares)


def force_kernel(pair, place_ref, airy_ref, *refs):
    if pair:
        *inner_refs, mine_ref, out_ref, total, weights = refs
    else:
        *inner_refs, out_ref, total, weights = refs
    n_k, rows, _ = inner_refs[0].shape
    half, core = place_ref[0], place_ref[1]
    weights[...] = airy_ref[...].astype(F32)

    for d, inner_ref in enumerate(inner_refs):
        acc = jnp.zeros((rows, WIDE), F32)
        for k in range(n_k):
            weight = weights[k : k + 1, d * WIDE : (d + 1) * WIDE]
            acc = acc + weight * inner_ref[k].astype(F32)
        at = pl.ds(pl.multiple_of(((half + d) % PARTS) * rows, rows), rows)
        total[at, :] = acc

    turned = total[...].T.reshape(N_SAME, FEW, PARTS * rows)
    turned = jnp.concatenate([turned[:, :8], turned[:, 8:]], axis=2).astype(BF)
    if pair:
        out_ref[:, core] = mine_ref[...]
        out_ref[:, 1 - core] = turned
    else:
        out_ref[...] = turned


def forces(place, airy, inners, mine=None):
    n_k, rows, _ = inners[0].shape
    pair = mine is not None
    shape = (N_SAME, 2, 8, 128) if pair else (N_SAME, 8, 128)
    operands = [airy, *inners] + ([mine] if pair else [])
    return pl.pallas_call(
        functools.partial(force_kernel, pair),
        in_specs=[pl.BlockSpec(memory_space=pltpu.SMEM)] + [VMEM] * len(operands),
        out_specs=VMEM,
        out_shape=jax.ShapeDtypeStruct(shape, BF),
        scratch_shapes=[pltpu.VMEM((PARTS * rows, WIDE), F32), pltpu.VMEM(airy.shape, F32)],
        cost_estimate=pl.CostEstimate(
            flops=2 * n_k * rows * airy.shape[1], bytes_accessed=4 << 20, transcendentals=0
        ),
        compiler_params=pltpu.CompilerParams(vmem_limit_bytes=8 << 20),
        name="forces",
    )(place, *[in_vmem(x) for x in operands])


def airy_kernel(place_ref, mine_ref, theirs_ref, out_ref):
    half, core = place_ref[0], place_ref[1]
    for source, at in ((mine_ref, core), (theirs_ref, 1 - core)):
        for d in range(PARTS):
            piece = source[:, d * WIDE : (d + 1) * WIDE].astype(F32).T
            out_ref[:, at, (half + d) % PARTS] = piece.reshape(N_SAME, FEW, piece.shape[1])


def airy_output(place, mine, theirs):
    full = pl.BlockSpec(mine.shape, lambda i, s: (0, 0))
    shape = (N_SAME, 2, PARTS, FEW, mine.shape[0])
    return pl.pallas_call(
        airy_kernel,
        grid_spec=pltpu.PrefetchScalarGridSpec(
            num_scalar_prefetch=1,
            grid=(1,),
            in_specs=[full, full],
            out_specs=pl.BlockSpec(shape, lambda i, s: (0,) * 5),
        ),
        out_shape=jax.ShapeDtypeStruct(shape, F32),
        cost_estimate=pl.CostEstimate(flops=1 << 20, bytes_accessed=1 << 20, transcendentals=0),
        compiler_params=pltpu.CompilerParams(vmem_limit_bytes=8 << 20),
        name="airy_output",
    )(place, mine, theirs)


def final_kernel(parts_ref, base_ref, damping_ref, out_ref):
    total = parts_ref[0].astype(F32)
    for i in range(1, parts_ref.shape[0]):
        total = total + parts_ref[i].astype(F32)
    scale = 1.0 + damping_ref[...]
    for a in range(4):
        rows = slice(8 * a, 8 * a + 8)
        at = (a % 2) * 64 + (a // 2) * 32
        force = jnp.concatenate([total[r][:, at : at + 32] for r in range(2 * N_SAME)], axis=1)
        out_ref[rows, :] = (base_ref[rows, :] - force) / scale


def final_step(parts, base, damping):
    return pl.pallas_call(
        final_kernel,
        out_shape=jax.ShapeDtypeStruct(base.shape, F32),
        compiler_params=pltpu.CompilerParams(vmem_limit_bytes=16 << 20),
        name="final_step",
    )(parts, base, damping)


def exchange(x, axes):
    return lax.all_to_all(x, axes, split_axis=0, concat_axis=0, tiled=True)


def spread(x, axes, n):
    return exchange(jnp.broadcast_to(x[None], (n, *x.shape)), axes)


def swap(x):
    return lax.ppermute(x, "c", [(0, 1), (1, 0)])


def shift(x, by):
    return lax.ppermute(x, "y", [(i, (i + by) % N_Y) for i in range(N_Y)])


def after(x):
    return lax.optimization_barrier(x)


def shards(
    amplitudes, previous, coupling, stiffness, airy_scale, damping, strike_mode, strike_offset
):
    n_k, rows, width = coupling.shape
    y = lax.axis_index("y").astype(jnp.int32)
    core = lax.axis_index("c").astype(jnp.int32)
    row = lax.axis_index(ROW).astype(jnp.int32).reshape(1)
    half = y % PARTS
    place = jnp.stack([half, core])

    per = n_k // N_SAME
    n_half = PARTS * WIDE
    row, place = after((row, place))
    piece = lax.dynamic_slice_in_dim(amplitudes, half * FEW, FEW, 0).astype(BF)
    piece, row, place = after((piece, row, place))
    b0 = spread(piece, SAME, N_SAME).reshape(WIDE, width)
    b0 = split(b0)
    b1 = [shift(b0[0], -1), shift(b0[1], 1)]
    o0 = [swap(b) for b in b0]
    (i0, j0), (p0, q0) = inner_products(row, coupling, [b0, o0], [F32, BF])

    b1, p0, q0 = after((b1, p0, q0))
    o1 = [swap(b) for b in b1]
    (i1,), (p1,) = inner_products(row, coupling, [b1], [F32], 64)

    o1, p1 = after((o1, p1))
    (j1,), (q1,) = inner_products(row, coupling, [o1], [BF], 64)

    part = combine(airy_scale, [p0, p1], [swap(q0), swap(q1)])
    shares = exchange(part.reshape(N_SAME, per, n_half), SAME)
    airy_own = exchange(total_everywhere(shares), SAME).reshape(n_k, n_half)
    airy_other = swap(airy_own)

    force_own = forces(place, airy_own, [i0, i1])
    messages = forces(place, airy_other, [j0, j1], force_own)
    messages, late = after((messages, (amplitudes, previous, damping, stiffness, strike_mode, strike_offset)))
    amplitudes, previous, damping, stiffness, strike_mode, strike_offset = late
    arrived = exchange(messages.reshape(2 * N_SAME, 8, 128), ROW)
    airy = airy_output(place, airy_own, airy_other).reshape(2 * N_SAME * rows, n_k)

    offset = strike_offset.astype(F32)
    pulse = jnp.where(
        strike_offset <= STRIKE_LEN, 2.0 * (1.0 - jnp.cos(jnp.pi * offset / STRIKE_LEN)), 0.0
    )
    modes = jnp.arange(width, dtype=jnp.int32)
    excite = jnp.where(modes[None, :] == strike_mode[:, None], pulse[:, None], 0.0)
    base = 2.0 * amplitudes - (1.0 - damping) * previous - stiffness * amplitudes + excite

    arrived, airy, base = after((arrived, airy, base))
    parts = spread(arrived, INPLANE, N_IN)
    result = final_step(parts, base, damping[None, :])
    return (result, airy)


def solution(mesh):
    fine = Mesh(mesh.devices.reshape(SIZES), AXES)
    return jax.shard_map(
        shards,
        mesh=fine,
        in_specs=(
            P(ROW, None),
            P(ROW, None),
            P(INPLANE, ROW, None),
            P(),
            P(INPLANE),
            P(),
            P(ROW),
            P(ROW),
        ),
        out_specs=(P(ROW, None), P(None, INPLANE)),
        check_vma=False,
    )
```

```python
import functools

import jax
import jax.numpy as jnp
from jax import lax
from jax.experimental import pallas as pl
from jax.experimental.pallas import tpu as pltpu
from jax.sharding import Mesh, PartitionSpec as P

STRIKE_LEN = 64
AXES = ("xh", "y", "xl", "z", "c")
SIZES = (2, 4, 2, 8, 2)
INPLANE = ("xh", "y")
ROW = ("xl", "z", "c")
SAME = ("xl", "z")
N_IN = 8
N_Y = 4
N_SAME = 16
PARTS = 2
FEW = 16
WIDE = 256
BF = jnp.bfloat16
F32 = jnp.float32


VMEM = pl.BlockSpec(memory_space=pltpu.VMEM)


def in_vmem(x):
    return pltpu.with_memory_space_constraint(x, pltpu.VMEM)


def inner_kernel(counts, slabs, stream, row_ref, tensor_ref, *refs):
    n_in, blocks = sum(counts), len(counts)
    case_refs = refs[:n_in]
    inner_refs = refs[n_in : n_in + blocks]
    part_refs = refs[n_in + blocks : n_in + 2 * blocks]
    turned = refs[-1]
    _, rows, width = tensor_ref.shape
    step = pl.program_id(0)

    @pl.when(step == 0)
    def _():
        at = 0
        for b, count in enumerate(counts):
            pieces = [case_refs[at + i][...] for i in range(count)]
            whole = pieces[0] if count == 1 else jnp.concatenate(pieces, axis=0)
            turned[:, b * WIDE : (b + 1) * WIDE] = whole.T
            at += count

    start = pl.multiple_of(row_ref[0] * rows, rows)
    columns = turned[pl.ds(start, rows), :].astype(F32)
    tensor = tensor_ref[...] if stream else tensor_ref[pl.ds(step * slabs, slabs)]
    inner = jnp.dot(
        tensor.reshape(slabs * rows, width), turned[...], preferred_element_type=F32
    ).reshape(slabs, rows, blocks * WIDE)
    for b in range(blocks):
        span = slice(b * WIDE, (b + 1) * WIDE)
        piece = inner[:, :, span]
        inner_refs[b][...] = piece.astype(BF)
        part = jnp.sum(piece * columns[None, :, span], axis=1)
        at = pl.ds(pl.multiple_of(step * slabs, slabs), slabs)
        part_refs[b][at, :] = part.astype(part_refs[b].dtype)


def inner_products(row, coupling, groups, part_types, slabs=32, stream=False):
    n_k, rows, width = coupling.shape
    counts = tuple(len(g) for g in groups)
    cases = [c for g in groups for c in g]
    blocks = len(groups)
    placed = pltpu.with_memory_space_constraint(coupling, pltpu.HBM if stream else pltpu.VMEM)
    out = pl.pallas_call(
        functools.partial(inner_kernel, counts, slabs, stream),
        grid_spec=pltpu.PrefetchScalarGridSpec(
            num_scalar_prefetch=1,
            grid=(n_k // slabs,),
            in_specs=[pl.BlockSpec((slabs, rows, width), lambda k, r: (k, 0, 0)) if stream else VMEM]
            + [VMEM] * len(cases),
            out_specs=[pl.BlockSpec((slabs, rows, WIDE), lambda k, r: (k, 0, 0))] * blocks
            + [VMEM] * blocks,
            scratch_shapes=[pltpu.VMEM((width, blocks * WIDE), BF)],
        ),
        out_shape=[jax.ShapeDtypeStruct((n_k, rows, WIDE), BF)] * blocks
        + [jax.ShapeDtypeStruct((n_k, WIDE), t) for t in part_types],
        cost_estimate=pl.CostEstimate(
            flops=2 * n_k * rows * width * blocks * WIDE, bytes_accessed=10 << 20, transcendentals=0
        ),
        compiler_params=pltpu.CompilerParams(vmem_limit_bytes=20 << 20),
        name="inner_products",
    )(row, placed, *[in_vmem(c) for c in cases])
    return out[:blocks], out[blocks:]


def split_kernel(whole_ref, *out_refs):
    for i, out_ref in enumerate(out_refs):
        out_ref[...] = whole_ref[i * WIDE // 2 : (i + 1) * WIDE // 2, :]


def split(whole):
    half = jax.ShapeDtypeStruct((WIDE // 2, whole.shape[1]), BF)
    return pl.pallas_call(
        split_kernel,
        in_specs=[VMEM],
        out_specs=[VMEM] * 2,
        out_shape=[half] * 2,
        cost_estimate=pl.CostEstimate(flops=1 << 34, bytes_accessed=1 << 20, transcendentals=0),
        compiler_params=pltpu.CompilerParams(vmem_limit_bytes=4 << 20),
        name="split",
    )(whole)


def combine_kernel(scale_ref, *refs):
    *sources, out_ref = refs
    half = len(sources) // 2
    n_k = out_ref.shape[0]
    scale = jnp.broadcast_to(scale_ref[...], (n_k, n_k)).T
    scale = jnp.concatenate([scale] * (WIDE // n_k), axis=1)
    for b in range(half):
        total = sources[b][...] + sources[half + b][...].astype(F32)
        out_ref[:, b * WIDE : (b + 1) * WIDE] = (total / scale).astype(BF)


def combine(airy_scale, mine, received):
    n_k = mine[0].shape[0]
    return pl.pallas_call(
        combine_kernel,
        out_shape=jax.ShapeDtypeStruct((n_k, WIDE * len(mine)), BF),
        compiler_params=pltpu.CompilerParams(vmem_limit_bytes=4 << 20),
        name="combine",
    )(airy_scale[None, :], *mine, *received)


def total_kernel(shares_ref, out_ref):
    total = shares_ref[0].astype(F32)
    for g in range(1, N_SAME):
        total = total + shares_ref[g].astype(F32)
    total = total.astype(BF)
    for g in range(N_SAME):
        out_ref[g] = total


def total_everywhere(shares):
    return pl.pallas_call(
        total_kernel,
        out_shape=jax.ShapeDtypeStruct(shares.shape, BF),
        compiler_params=pltpu.CompilerParams(vmem_limit_bytes=4 << 20),
        name="total_everywhere",
    )(shares)


def force_kernel(pair, place_ref, airy_ref, *refs):
    if pair:
        *inner_refs, mine_ref, out_ref, total, weights = refs
    else:
        *inner_refs, out_ref, total, weights = refs
    n_k, rows, _ = inner_refs[0].shape
    half, core = place_ref[0], place_ref[1]
    weights[...] = airy_ref[...].astype(F32)

    for d, inner_ref in enumerate(inner_refs):
        acc = jnp.zeros((rows, WIDE), F32)
        for k in range(n_k):
            weight = weights[k : k + 1, d * WIDE : (d + 1) * WIDE]
            acc = acc + weight * inner_ref[k].astype(F32)
        at = pl.ds(pl.multiple_of(((half + d) % PARTS) * rows, rows), rows)
        total[at, :] = acc

    turned = total[...].T.reshape(N_SAME, FEW, PARTS * rows)
    turned = jnp.concatenate([turned[:, :8], turned[:, 8:]], axis=2).astype(BF)
    if pair:
        out_ref[:, core] = mine_ref[...]
        out_ref[:, 1 - core] = turned
    else:
        out_ref[...] = turned


def forces(place, airy, inners, mine=None):
    n_k, rows, _ = inners[0].shape
    pair = mine is not None
    shape = (N_SAME, 2, 8, 128) if pair else (N_SAME, 8, 128)
    operands = [airy, *inners] + ([mine] if pair else [])
    return pl.pallas_call(
        functools.partial(force_kernel, pair),
        in_specs=[pl.BlockSpec(memory_space=pltpu.SMEM)] + [VMEM] * len(operands),
        out_specs=VMEM,
        out_shape=jax.ShapeDtypeStruct(shape, BF),
        scratch_shapes=[pltpu.VMEM((PARTS * rows, WIDE), F32), pltpu.VMEM(airy.shape, F32)],
        cost_estimate=pl.CostEstimate(
            flops=2 * n_k * rows * airy.shape[1], bytes_accessed=4 << 20, transcendentals=0
        ),
        compiler_params=pltpu.CompilerParams(vmem_limit_bytes=8 << 20),
        name="forces",
    )(place, *[in_vmem(x) for x in operands])


def airy_kernel(place_ref, mine_ref, theirs_ref, out_ref):
    half, core = place_ref[0], place_ref[1]
    for source, at in ((mine_ref, core), (theirs_ref, 1 - core)):
        for d in range(PARTS):
            piece = source[:, d * WIDE : (d + 1) * WIDE].astype(F32).T
            out_ref[:, at, (half + d) % PARTS] = piece.reshape(N_SAME, FEW, piece.shape[1])


def airy_output(place, mine, theirs):
    full = pl.BlockSpec(mine.shape, lambda i, s: (0, 0))
    shape = (N_SAME, 2, PARTS, FEW, mine.shape[0])
    return pl.pallas_call(
        airy_kernel,
        grid_spec=pltpu.PrefetchScalarGridSpec(
            num_scalar_prefetch=1,
            grid=(1,),
            in_specs=[full, full],
            out_specs=pl.BlockSpec(shape, lambda i, s: (0,) * 5),
        ),
        out_shape=jax.ShapeDtypeStruct(shape, F32),
        cost_estimate=pl.CostEstimate(flops=1 << 20, bytes_accessed=1 << 20, transcendentals=0),
        compiler_params=pltpu.CompilerParams(vmem_limit_bytes=8 << 20),
        name="airy_output",
    )(place, mine, theirs)


def final_kernel(parts_ref, base_ref, damping_ref, out_ref):
    total = parts_ref[0].astype(F32)
    for i in range(1, parts_ref.shape[0]):
        total = total + parts_ref[i].astype(F32)
    scale = 1.0 + damping_ref[...]
    for a in range(4):
        rows = slice(8 * a, 8 * a + 8)
        at = (a % 2) * 64 + (a // 2) * 32
        force = jnp.concatenate([total[r][:, at : at + 32] for r in range(2 * N_SAME)], axis=1)
        out_ref[rows, :] = (base_ref[rows, :] - force) / scale


def final_step(parts, base, damping):
    return pl.pallas_call(
        final_kernel,
        out_shape=jax.ShapeDtypeStruct(base.shape, F32),
        compiler_params=pltpu.CompilerParams(vmem_limit_bytes=16 << 20),
        name="final_step",
    )(parts, base, damping)


def exchange(x, axes):
    return lax.all_to_all(x, axes, split_axis=0, concat_axis=0, tiled=True)


def spread(x, axes, n):
    return exchange(jnp.broadcast_to(x[None], (n, *x.shape)), axes)


def swap(x):
    return lax.ppermute(x, "c", [(0, 1), (1, 0)])


def shift(x, by):
    return lax.ppermute(x, "y", [(i, (i + by) % N_Y) for i in range(N_Y)])


def after(x):
    return lax.optimization_barrier(x)


def shards(
    amplitudes, previous, coupling, stiffness, airy_scale, damping, strike_mode, strike_offset
):
    n_k, rows, width = coupling.shape
    y = lax.axis_index("y").astype(jnp.int32)
    core = lax.axis_index("c").astype(jnp.int32)
    row = lax.axis_index(ROW).astype(jnp.int32).reshape(1)
    half = y % PARTS
    place = jnp.stack([half, core])

    per = n_k // N_SAME
    n_half = PARTS * WIDE
    row, place = after((row, place))
    piece = lax.dynamic_slice_in_dim(amplitudes, half * FEW, FEW, 0).astype(BF)
    piece, row, place = after((piece, row, place))
    b0 = spread(piece, SAME, N_SAME).reshape(WIDE, width)
    o0 = swap(b0)
    b1 = [shift(b, by) for b, by in zip(split(b0), (-1, 1))]
    (i0, j0), (p0, q0) = inner_products(row, coupling, [[b0], [o0]], [F32, BF])

    b1, p0, q0 = after((b1, p0, q0))
    o1 = [swap(b) for b in b1]
    (i1,), (p1,) = inner_products(row, coupling, [b1], [F32], 64)

    o1, p1 = after((o1, p1))
    (j1,), (q1,) = inner_products(row, coupling, [o1], [BF], 64)

    part = combine(airy_scale, [p0, p1], [swap(q0), swap(q1)])
    shares = exchange(part.reshape(N_SAME, per, n_half), SAME)
    airy_own = exchange(total_everywhere(shares), SAME).reshape(n_k, n_half)
    airy_other = swap(airy_own)

    force_own = forces(place, airy_own, [i0, i1])
    messages = forces(place, airy_other, [j0, j1], force_own)
    messages, late = after((messages, (amplitudes, previous, damping, stiffness, strike_mode, strike_offset)))
    amplitudes, previous, damping, stiffness, strike_mode, strike_offset = late
    arrived = exchange(messages.reshape(2 * N_SAME, 8, 128), ROW)
    airy = airy_output(place, airy_own, airy_other).reshape(2 * N_SAME * rows, n_k)

    offset = strike_offset.astype(F32)
    pulse = jnp.where(
        strike_offset <= STRIKE_LEN, 2.0 * (1.0 - jnp.cos(jnp.pi * offset / STRIKE_LEN)), 0.0
    )
    modes = jnp.arange(width, dtype=jnp.int32)
    excite = jnp.where(modes[None, :] == strike_mode[:, None], pulse[:, None], 0.0)
    base = 2.0 * amplitudes - (1.0 - damping) * previous - stiffness * amplitudes + excite

    arrived, airy, base = after((arrived, airy, base))
    parts = spread(arrived, INPLANE, N_IN)
    result = final_step(parts, base, damping[None, :])
    return (result, airy)


def solution(mesh):
    fine = Mesh(mesh.devices.reshape(SIZES), AXES)
    return jax.shard_map(
        shards,
        mesh=fine,
        in_specs=(
            P(ROW, None),
            P(ROW, None),
            P(INPLANE, ROW, None),
            P(),
            P(INPLANE),
            P(),
            P(ROW),
            P(ROW),
        ),
        out_specs=(P(ROW, None), P(None, INPLANE)),
        check_vma=False,
    )
```

```python
import functools

import jax
import jax.numpy as jnp
from jax import lax
from jax.experimental import pallas as pl
from jax.experimental.pallas import tpu as pltpu
from jax.sharding import Mesh, PartitionSpec as P

STRIKE_LEN = 64
AXES = ("xh", "y", "xl", "z", "c")
SIZES = (2, 4, 2, 8, 2)
INPLANE = ("xh", "y")
ROW = ("xl", "z", "c")
SAME = ("xl", "z")
N_IN = 8
N_Y = 4
N_SAME = 16
PARTS = 2
FEW = 16
WIDE = 256
BF = jnp.bfloat16
F32 = jnp.float32


VMEM = pl.BlockSpec(memory_space=pltpu.VMEM)


def in_vmem(x):
    return pltpu.with_memory_space_constraint(x, pltpu.VMEM)


def inner_kernel(counts, slabs, stream, row_ref, tensor_ref, *refs):
    n_in, blocks = sum(counts), len(counts)
    case_refs = refs[:n_in]
    inner_refs = refs[n_in : n_in + blocks]
    part_refs = refs[n_in + blocks : n_in + 2 * blocks]
    turned = refs[-1]
    _, rows, width = tensor_ref.shape
    step = pl.program_id(0)

    @pl.when(step == 0)
    def _():
        at = 0
        for b, count in enumerate(counts):
            pieces = [case_refs[at + i][...] for i in range(count)]
            whole = pieces[0] if count == 1 else jnp.concatenate(pieces, axis=0)
            turned[:, b * WIDE : (b + 1) * WIDE] = whole.T
            at += count

    start = pl.multiple_of(row_ref[0] * rows, rows)
    columns = turned[pl.ds(start, rows), :].astype(F32)
    tensor = tensor_ref[...] if stream else tensor_ref[pl.ds(step * slabs, slabs)]
    inner = jnp.dot(
        tensor.reshape(slabs * rows, width), turned[...], preferred_element_type=F32
    ).reshape(slabs, rows, blocks * WIDE)
    for b in range(blocks):
        span = slice(b * WIDE, (b + 1) * WIDE)
        piece = inner[:, :, span]
        inner_refs[b][...] = piece.astype(BF)
        part = jnp.sum(piece * columns[None, :, span], axis=1)
        at = pl.ds(pl.multiple_of(step * slabs, slabs), slabs)
        part_refs[b][at, :] = part.astype(part_refs[b].dtype)


def inner_products(row, coupling, groups, part_types, slabs=32, stream=False):
    n_k, rows, width = coupling.shape
    counts = tuple(len(g) for g in groups)
    cases = [c for g in groups for c in g]
    blocks = len(groups)
    placed = pltpu.with_memory_space_constraint(coupling, pltpu.HBM if stream else pltpu.VMEM)
    out = pl.pallas_call(
        functools.partial(inner_kernel, counts, slabs, stream),
        grid_spec=pltpu.PrefetchScalarGridSpec(
            num_scalar_prefetch=1,
            grid=(n_k // slabs,),
            in_specs=[pl.BlockSpec((slabs, rows, width), lambda k, r: (k, 0, 0)) if stream else VMEM]
            + [VMEM] * len(cases),
            out_specs=[pl.BlockSpec((slabs, rows, WIDE), lambda k, r: (k, 0, 0))] * blocks
            + [VMEM] * blocks,
            scratch_shapes=[pltpu.VMEM((width, blocks * WIDE), BF)],
        ),
        out_shape=[jax.ShapeDtypeStruct((n_k, rows, WIDE), BF)] * blocks
        + [jax.ShapeDtypeStruct((n_k, WIDE), t) for t in part_types],
        cost_estimate=pl.CostEstimate(
            flops=2 * n_k * rows * width * blocks * WIDE, bytes_accessed=10 << 20, transcendentals=0
        ),
        compiler_params=pltpu.CompilerParams(vmem_limit_bytes=20 << 20),
        name="inner_products",
    )(row, placed, *[in_vmem(c) for c in cases])
    return out[:blocks], out[blocks:]


def split_kernel(whole_ref, *out_refs):
    for i, out_ref in enumerate(out_refs):
        out_ref[...] = whole_ref[i * WIDE // 2 : (i + 1) * WIDE // 2, :]


def split(whole):
    half = jax.ShapeDtypeStruct((WIDE // 2, whole.shape[1]), BF)
    return pl.pallas_call(
        split_kernel,
        in_specs=[VMEM],
        out_specs=[VMEM] * 2,
        out_shape=[half] * 2,
        cost_estimate=pl.CostEstimate(flops=1 << 34, bytes_accessed=1 << 20, transcendentals=0),
        compiler_params=pltpu.CompilerParams(vmem_limit_bytes=4 << 20),
        name="split",
    )(whole)


def combine_kernel(scale_ref, *refs):
    *sources, out_ref = refs
    half = len(sources) // 2
    n_k = out_ref.shape[0]
    scale = jnp.broadcast_to(scale_ref[...], (n_k, n_k)).T
    scale = jnp.concatenate([scale] * (WIDE // n_k), axis=1)
    for b in range(half):
        total = sources[b][...] + sources[half + b][...].astype(F32)
        out_ref[:, b * WIDE : (b + 1) * WIDE] = (total / scale).astype(BF)


def combine(airy_scale, mine, received):
    n_k = mine[0].shape[0]
    return pl.pallas_call(
        combine_kernel,
        out_shape=jax.ShapeDtypeStruct((n_k, WIDE * len(mine)), BF),
        compiler_params=pltpu.CompilerParams(vmem_limit_bytes=4 << 20),
        name="combine",
    )(airy_scale[None, :], *mine, *received)


def total_kernel(shares_ref, out_ref):
    total = shares_ref[0].astype(F32)
    for g in range(1, N_SAME):
        total = total + shares_ref[g].astype(F32)
    total = total.astype(BF)
    for g in range(N_SAME):
        out_ref[g] = total


def total_everywhere(shares):
    return pl.pallas_call(
        total_kernel,
        out_shape=jax.ShapeDtypeStruct(shares.shape, BF),
        compiler_params=pltpu.CompilerParams(vmem_limit_bytes=4 << 20),
        name="total_everywhere",
    )(shares)


def force_kernel(pair, place_ref, airy_ref, *refs):
    if pair:
        *inner_refs, mine_ref, out_ref, total, weights = refs
    else:
        *inner_refs, out_ref, total, weights = refs
    n_k, rows, _ = inner_refs[0].shape
    half, core = place_ref[0], place_ref[1]
    weights[...] = airy_ref[...].astype(F32)

    for d, inner_ref in enumerate(inner_refs):
        acc = jnp.zeros((rows, WIDE), F32)
        for k in range(n_k):
            weight = weights[k : k + 1, d * WIDE : (d + 1) * WIDE]
            acc = acc + weight * inner_ref[k].astype(F32)
        at = pl.ds(pl.multiple_of(((half + d) % PARTS) * rows, rows), rows)
        total[at, :] = acc

    turned = total[...].T.reshape(N_SAME, FEW, PARTS * rows)
    turned = jnp.concatenate([turned[:, :8], turned[:, 8:]], axis=2).astype(BF)
    if pair:
        out_ref[:, core] = mine_ref[...]
        out_ref[:, 1 - core] = turned
    else:
        out_ref[...] = turned


def forces(place, airy, inners, mine=None):
    n_k, rows, _ = inners[0].shape
    pair = mine is not None
    shape = (N_SAME, 2, 8, 128) if pair else (N_SAME, 8, 128)
    operands = [airy, *inners] + ([mine] if pair else [])
    return pl.pallas_call(
        functools.partial(force_kernel, pair),
        in_specs=[pl.BlockSpec(memory_space=pltpu.SMEM)] + [VMEM] * len(operands),
        out_specs=VMEM,
        out_shape=jax.ShapeDtypeStruct(shape, BF),
        scratch_shapes=[pltpu.VMEM((PARTS * rows, WIDE), F32), pltpu.VMEM(airy.shape, F32)],
        cost_estimate=pl.CostEstimate(
            flops=2 * n_k * rows * airy.shape[1], bytes_accessed=4 << 20, transcendentals=0
        ),
        compiler_params=pltpu.CompilerParams(vmem_limit_bytes=8 << 20),
        name="forces",
    )(place, *[in_vmem(x) for x in operands])


def airy_kernel(place_ref, mine_ref, theirs_ref, out_ref):
    half, core = place_ref[0], place_ref[1]
    for source, at in ((mine_ref, core), (theirs_ref, 1 - core)):
        for d in range(PARTS):
            piece = source[:, d * WIDE : (d + 1) * WIDE].astype(F32).T
            out_ref[:, at, (half + d) % PARTS] = piece.reshape(N_SAME, FEW, piece.shape[1])


def airy_output(place, mine, theirs):
    full = pl.BlockSpec(mine.shape, lambda i, s: (0, 0))
    shape = (N_SAME, 2, PARTS, FEW, mine.shape[0])
    return pl.pallas_call(
        airy_kernel,
        grid_spec=pltpu.PrefetchScalarGridSpec(
            num_scalar_prefetch=1,
            grid=(1,),
            in_specs=[full, full],
            out_specs=pl.BlockSpec(shape, lambda i, s: (0,) * 5),
        ),
        out_shape=jax.ShapeDtypeStruct(shape, F32),
        cost_estimate=pl.CostEstimate(flops=1 << 20, bytes_accessed=1 << 20, transcendentals=0),
        compiler_params=pltpu.CompilerParams(vmem_limit_bytes=8 << 20),
        name="airy_output",
    )(place, mine, theirs)


def final_kernel(parts_ref, base_ref, damping_ref, out_ref):
    total = parts_ref[0].astype(F32)
    for i in range(1, parts_ref.shape[0]):
        total = total + parts_ref[i].astype(F32)
    scale = 1.0 + damping_ref[...]
    for a in range(4):
        rows = slice(8 * a, 8 * a + 8)
        at = (a % 2) * 64 + (a // 2) * 32
        force = jnp.concatenate([total[r][:, at : at + 32] for r in range(2 * N_SAME)], axis=1)
        out_ref[rows, :] = (base_ref[rows, :] - force) / scale


def final_step(parts, base, damping):
    return pl.pallas_call(
        final_kernel,
        out_shape=jax.ShapeDtypeStruct(base.shape, F32),
        compiler_params=pltpu.CompilerParams(vmem_limit_bytes=16 << 20),
        name="final_step",
    )(parts, base, damping)


def exchange(x, axes):
    return lax.all_to_all(x, axes, split_axis=0, concat_axis=0, tiled=True)


def spread(x, axes, n):
    return exchange(jnp.broadcast_to(x[None], (n, *x.shape)), axes)


def swap(x):
    return lax.ppermute(x, "c", [(0, 1), (1, 0)])


def shift(x, by):
    return lax.ppermute(x, "y", [(i, (i + by) % N_Y) for i in range(N_Y)])


def after(x):
    return lax.optimization_barrier(x)


def shards(
    amplitudes, previous, coupling, stiffness, airy_scale, damping, strike_mode, strike_offset
):
    n_k, rows, width = coupling.shape
    y = lax.axis_index("y").astype(jnp.int32)
    core = lax.axis_index("c").astype(jnp.int32)
    row = lax.axis_index(ROW).astype(jnp.int32).reshape(1)
    half = y % PARTS
    place = jnp.stack([half, core])

    per = n_k // N_SAME
    n_half = PARTS * WIDE
    row, place = after((row, place))
    piece = lax.dynamic_slice_in_dim(amplitudes, half * FEW, FEW, 0).astype(BF)
    piece, row, place = after((piece, row, place))
    b0 = spread(piece, SAME, N_SAME).reshape(WIDE, width)
    o0 = swap(b0)
    b1 = [shift(b, by) for b, by in zip(split(b0), (-1, 1))]
    (i0, j0), (p0, q0) = inner_products(row, coupling, [[b0], [o0]], [F32, BF], 64)

    b1, p0, q0 = after((b1, p0, q0))
    o1 = [swap(b) for b in b1]
    (i1,), (p1,) = inner_products(row, coupling, [b1], [F32], 64)

    o1, p1 = after((o1, p1))
    (j1,), (q1,) = inner_products(row, coupling, [o1], [BF], 64)

    part = combine(airy_scale, [p0, p1], [swap(q0), swap(q1)])
    shares = exchange(part.reshape(N_SAME, per, n_half), SAME)
    airy_own = exchange(total_everywhere(shares), SAME).reshape(n_k, n_half)
    airy_other = swap(airy_own)

    force_own = forces(place, airy_own, [i0, i1])
    messages = forces(place, airy_other, [j0, j1], force_own)
    messages, late = after((messages, (amplitudes, previous, damping, stiffness, strike_mode, strike_offset)))
    amplitudes, previous, damping, stiffness, strike_mode, strike_offset = late
    arrived = exchange(messages.reshape(2 * N_SAME, 8, 128), ROW)
    airy = airy_output(place, airy_own, airy_other).reshape(2 * N_SAME * rows, n_k)

    offset = strike_offset.astype(F32)
    pulse = jnp.where(
        strike_offset <= STRIKE_LEN, 2.0 * (1.0 - jnp.cos(jnp.pi * offset / STRIKE_LEN)), 0.0
    )
    modes = jnp.arange(width, dtype=jnp.int32)
    excite = jnp.where(modes[None, :] == strike_mode[:, None], pulse[:, None], 0.0)
    base = 2.0 * amplitudes - (1.0 - damping) * previous - stiffness * amplitudes + excite

    arrived, airy, base = after((arrived, airy, base))
    parts = spread(arrived, INPLANE, N_IN)
    result = final_step(parts, base, damping[None, :])
    return (result, airy)


def solution(mesh):
    fine = Mesh(mesh.devices.reshape(SIZES), AXES)
    return jax.shard_map(
        shards,
        mesh=fine,
        in_specs=(
            P(ROW, None),
            P(ROW, None),
            P(INPLANE, ROW, None),
            P(),
            P(INPLANE),
            P(),
            P(ROW),
            P(ROW),
        ),
        out_specs=(P(ROW, None), P(None, INPLANE)),
        check_vma=False,
    )
```
